128 devices in a mesh: section: 8 (over x_hi, y), dp: 16 (over z, x_lo, core).
Axes of the slice: x: 4 (x_hi: 2, x_lo: 2; x = x_hi * 2 + x_lo), y: 4, z: 4, core: 2. Of those that a mesh axis runs over, the one named last changes fastest.
Arguments:
- acts_in: bfloat16 [2, 128, 6144], P(None, 'dp'), may hold values from -6 to 6
- weights: bfloat16 [8, 6144, 6144], P('section', None, 'dp'), may hold values from -0.078125 to 0.078125
- gains: float32 [8, 6144], P('section'), may hold values from 0.25 to 1.75
- stored: bfloat16 [8, 64, 8, 6144], P('section', 'dp'), may hold values from -6 to 6
- sample_ids: int32 [2, 16], P(None, 'dp'), may hold values from 0 to 63, as said below
- cotangent: bfloat16 [2, 128, 6144], P(None, 'dp'), may hold values from -0.1796875 to 0.1796875
Outputs:
- new_stored: bfloat16 [8, 64, 8, 6144], P('section', 'dp')
- grad_weight: float32 [8, 6144, 6144], P('section', None, 'dp')
- grad_gain: float32 [8, 6144], P('section')
The draws below stay inside these ranges and needn't reach their ends.
Inputs may be any that keep to these rules, and one draw needn't show every extreme that they name: `sample_ids`: column k names slots k * 4 to (k + 1) * 4 - 1 only, and the 2 micro-batches name different slots in each column.
All inputs are finite; a program needn't handle non-finite values.
Results may differ from the reference program's by a relative error of at most 0.04.
Values may be sent and summed in bfloat16 or wider, within the bound.
A program may use at most 704 MiB of HBM per device.

```python
import jax
import jax.numpy as jnp
from jax import lax

D = 6144
SEG = 8
MICRO = 2
BUF = 4
SECTIONS = 8
TOKENS = 128
SLOTS = 64
DC = 384
N_DP = 16


def forced_order(key, value):
    first, second = jax.random.split(key)
    others = jnp.arange(BUF - 1, dtype=jnp.int32)
    others = others + (others >= value).astype(jnp.int32)
    others = jax.random.permutation(first, others)
    padded = jnp.concatenate([others, jnp.zeros((1,), jnp.int32)])
    where_at = jax.random.randint(second, (), 0, MICRO)
    index = jnp.arange(BUF, dtype=jnp.int32)
    shifted = jnp.clip(index - 1, 0, BUF - 1)
    order = jnp.where(index < where_at, padded[index], jnp.where(index == where_at, value, padded[shifted]))
    return order.astype(jnp.int32)


def draw_sample_ids(key, part):
    key = jax.random.fold_in(key, 7)
    groups = SLOTS // BUF
    keys = jax.random.split(key, groups + 2)
    middle = jax.vmap(lambda single: jax.random.permutation(single, BUF))(keys[:groups]).astype(jnp.int32)
    first_row = forced_order(keys[groups], 0)
    last_row = forced_order(keys[groups + 1], BUF - 1)
    middle = middle.at[0].set(first_row)
    middle = middle.at[groups - 1].set(last_row)
    picks = middle[:, :MICRO]
    return (picks + jnp.arange(groups, dtype=jnp.int32)[:, None] * BUF).T.astype(jnp.int32)


def block_levels(stream_key, extent, pieces, low, high):
    factor_of, own = 1.0, jax.random.fold_in(stream_key, 6)
    for dim, parts in pieces:
        draws = jnp.exp(jax.random.uniform(jax.random.fold_in(own, dim), (parts,), jnp.float32, low / len(pieces), high / len(pieces)))
        factor_of = factor_of * jnp.repeat(draws, extent[dim] // parts).reshape([-1 if axis == dim else 1 for axis in range(len(extent))])
    return factor_of


def gaussian(rng, dims, scale, reach, pieces=(), held_as=jnp.bfloat16):
    values = scale * jax.random.normal(rng, dims, jnp.float32)
    if pieces:
        values = values * block_levels(rng, dims, pieces, -0.22, 0.18)
    return jnp.clip(values, -reach, reach).astype(held_as)


def setup_inputs(seed: int = 0) -> dict:
    splits = jax.random.split(jax.random.key(seed), 7)
    return {
        "acts_in": gaussian(splits[0], (MICRO, TOKENS, D), 1.0, 6.0, ((1, 16),)),
        "weights": gaussian(splits[1], (SECTIONS, D, D), D ** -0.5, 0.078125, ((0, 8), (2, 16))),
        "gains": jnp.clip(1.0 + 0.15 * jax.random.normal(splits[2], (SECTIONS, D), jnp.float32), 0.25, 1.75),
        "stored": gaussian(splits[3], (SECTIONS, SLOTS, SEG, D), 1.0, 6.0, ((0, 8), (1, 16))),
        "sample_ids": draw_sample_ids(jax.random.fold_in(splits[6], 71), 0),
        "cotangent": gaussian(splits[5], (MICRO, TOKENS, D), 0.03, 0.1796875, ((1, 16),)),
    }


clip_limit = 1.0
epsilon = 1e-05
gelu_coeff = 0.7978845608028654

def gelu_value(values):
    inner = gelu_coeff * (values + 0.044715 * values * values * values)
    return 0.5 * values * (1.0 + jnp.tanh(inner))

def gelu_slope(values):
    tangent = jnp.tanh(gelu_coeff * (values + 0.044715 * values * values * values))
    return 0.5 * (1.0 + tangent) + 0.5 * values * (1.0 - tangent * tangent) * gelu_coeff * (1.0 + 0.134145 * values * values)

def reference(acts_in, weights, gains, stored, sample_ids, cotangent):
    new_stored = stored
    records = []
    for micro_no in range(MICRO):
        incoming = acts_in[micro_no]
        saved = []
        for section_no in range(SECTIONS):
            previous = stored[section_no][sample_ids[micro_no]].reshape(TOKENS, D).astype(jnp.float32)
            moved = jnp.clip(incoming.astype(jnp.float32) - previous, -clip_limit, clip_limit)
            arrived = (previous + moved).astype(jnp.bfloat16)
            new_stored = new_stored.at[section_no, sample_ids[micro_no]].set(arrived.reshape(N_DP, SEG, D))
            arrived_f = arrived.astype(jnp.float32)
            scale_inv = lax.rsqrt(lax.optimization_barrier(jnp.mean(arrived_f * arrived_f, axis=-1, keepdims=True)) + epsilon)
            normed = (arrived_f * scale_inv * gains[section_no]).astype(jnp.bfloat16)
            hidden = jnp.dot(normed, weights[section_no], preferred_element_type=jnp.float32)
            incoming = (arrived_f + gelu_value(hidden)).astype(jnp.bfloat16)
            saved.append((arrived_f, scale_inv, normed, hidden))
        records.append(saved)
    grad_weight = jnp.zeros((SECTIONS, D, D), jnp.float32)
    grad_gain = jnp.zeros((SECTIONS, D), jnp.float32)
    for micro_no in range(MICRO):
        upstream = cotangent[micro_no]
        for section_no in reversed(range(SECTIONS)):
            arrived_f, scale_inv, normed, hidden = records[micro_no][section_no]
            slope = (upstream.astype(jnp.float32) * gelu_slope(hidden)).astype(jnp.bfloat16)
            grad_weight = grad_weight.at[section_no].add(jnp.dot(normed.T, slope, preferred_element_type=jnp.float32))
            blocks = jnp.einsum('tjc,djc->jtd', slope.astype(jnp.float32).reshape(TOKENS, N_DP, DC), weights[section_no].astype(jnp.float32).reshape(D, N_DP, DC))
            rounded = lax.optimization_barrier(blocks.astype(jnp.bfloat16))
            back_normed = lax.optimization_barrier(jnp.sum(rounded.astype(jnp.float32), axis=0))
            grad_gain = grad_gain.at[section_no].add(lax.optimization_barrier(jnp.sum(back_normed * arrived_f * scale_inv, axis=0)))
            weighted = back_normed * gains[section_no]
            mean_term = lax.optimization_barrier(jnp.mean(weighted * arrived_f, axis=-1, keepdims=True))
            total = upstream.astype(jnp.float32) + scale_inv * (weighted - arrived_f * scale_inv * scale_inv * mean_term)
            upstream = total.astype(jnp.bfloat16)
    return (new_stored, grad_weight, grad_gain)
```

```python
import functools

import jax
import jax.numpy as jnp
from jax import lax
from jax.experimental import pallas as pl
from jax.experimental.pallas import tpu as pltpu
from jax.sharding import PartitionSpec as P

MESH = pl.DeviceIdType.MESH
F32 = jnp.float32
BF16 = jnp.bfloat16

clip_limit = 1.0
epsilon = 1e-05
gelu_coeff = 0.7978845608028654


def gelu_value(values):
    inner = gelu_coeff * (values + 0.044715 * values * values * values)
    return 0.5 * values * (1.0 + jnp.tanh(inner))


def gelu_slope(values):
    tangent = jnp.tanh(gelu_coeff * (values + 0.044715 * values * values * values))
    return 0.5 * (1.0 + tangent) + 0.5 * values * (1.0 - tangent * tangent) * gelu_coeff * (
        1.0 + 0.134145 * values * values
    )


def relay(
    sections,
    groups,
    ids,
    acts,
    weights,
    gains,
    stored,
    cotangent,
    arrived_out,
    normed_out,
    slope_out,
    gain_out,
    wbuf,
    nbuf,
    gbuf,
    xbuf,
    pout,
    pin,
    hidden,
    hop_in,
    hop_out,
    slopes,
    slope_in,
    ybuf,
    back_out,
    back_in,
    up_in,
    up_out,
    scales,
    gain_sum,
    gain_row,
    gain_in,
    w_sem,
    send_sem,
    recv_sem,
    copy_sem,
    gain_sem,
):
    micro, seg_rows, width = acts.shape
    half = width // 2
    own_cols = weights.shape[2]
    chip_cols = 2 * own_cols
    chips = groups // 2
    rows = groups * seg_rows
    slot_count = stored.shape[1]
    section = lax.axis_index("section")
    me = lax.axis_index("dp")
    core = lax.rem(me, 2)
    sibling = me + 1 - 2 * core
    first = section == 0
    last = section == sections - 1
    gather_no, part_no, slope_no, back_no, hop_no, up_no, keep_no = range(7)

    barrier = pltpu.get_barrier_semaphore()

    def greet(step, carry):
        pl.semaphore_signal(
            barrier, inc=1, device_id={"dp": lax.rem(me + step, groups)}, device_id_type=MESH
        )
        return carry

    lax.fori_loop(1, groups, greet, 0)
    for other in (lax.rem(section + 1, sections), lax.rem(section + sections - 1, sections)):
        pl.semaphore_signal(barrier, inc=1, device_id={"section": other}, device_id_type=MESH)
    pl.semaphore_wait(barrier, groups + 1)

    own_place = pl.ds(pl.multiple_of(core * own_cols, 128), own_cols)

    def weight_share():
        return pltpu.make_async_remote_copy(
            src_ref=weights.at[0, pl.ds((1 - core) * half, half), :],
            dst_ref=wbuf.at[:, own_place],
            send_sem=w_sem.at[0],
            recv_sem=w_sem.at[1],
            device_id={"dp": sibling},
            device_id_type=MESH,
        )

    def weight_own():
        return pltpu.make_async_copy(
            weights.at[0, pl.ds(core * half, half), :], wbuf.at[:, own_place], w_sem.at[2]
        )

    weight_share().start()
    weight_own().start()

    def exchange(stage, m, source, target):
        def send(step, carry):
            other = lax.rem(me + step, groups)
            pltpu.make_async_remote_copy(
                src_ref=source(other),
                dst_ref=target.at[m, me],
                send_sem=send_sem.at[stage, m],
                recv_sem=recv_sem.at[stage, m],
                device_id={"dp": other},
                device_id_type=MESH,
            ).start()
            return carry

        lax.fori_loop(1, groups, send, 0)
        pltpu.make_async_copy(source(me), target.at[m, me], recv_sem.at[stage, m]).start()

    def await_all(stage, m, target):
        pltpu.make_async_copy(target.at[m], target.at[m], recv_sem.at[stage, m]).wait()

    def await_sent(stage, m, target):
        most = target.at[m, pl.ds(0, groups - 1)]
        pltpu.make_async_copy(most, most, send_sem.at[stage, m]).wait()

    def hop(stage, m, source, target, towards):
        return pltpu.make_async_remote_copy(
            src_ref=source.at[m],
            dst_ref=target.at[m],
            send_sem=send_sem.at[stage, m],
            recv_sem=recv_sem.at[stage, m],
            device_id={"section": towards},
            device_id_type=MESH,
        )

    def keep_copies(m):
        return (
            pltpu.make_async_remote_copy(
                src_ref=gbuf.at[m],
                dst_ref=normed_out.at[core, m],
                send_sem=send_sem.at[keep_no, m],
                recv_sem=recv_sem.at[keep_no, m],
                device_id={"dp": sibling},
                device_id_type=MESH,
            ),
            pltpu.make_async_copy(gbuf.at[m], normed_out.at[core, m], copy_sem.at[0, m]),
        )

    def slope_copy(m):
        return pltpu.make_async_copy(
            slope_in.at[m, :, :, own_place], slope_out.at[m], copy_sem.at[1, m]
        )

    after = lax.rem(section + 1, sections)
    before = lax.rem(section + sections - 1, sections)
    step_k = 512

    def forward(m, carry):
        @pl.when(first)
        def _():
            hop_in[m] = acts[m]

        @pl.when(jnp.logical_not(first))
        def _():
            hop(hop_no, m, hop_out, hop_in, after).wait_recv()

        slot = jnp.clip(ids[m, 0] - me * slot_count, 0, slot_count - 1)
        previous = stored[0, slot].astype(F32)
        moved = jnp.clip(hop_in[m].astype(F32) - previous, -clip_limit, clip_limit)
        arrived = (previous + moved).astype(BF16)
        arrived_out[m] = arrived
        arrived_f = arrived.astype(F32)
        scale = lax.rsqrt(jnp.mean(arrived_f * arrived_f, axis=-1, keepdims=True) + epsilon)
        scales[m] = jnp.broadcast_to(scale, (seg_rows, 128))
        normed = (arrived_f * scale * gains[...]).astype(BF16)
        nbuf[m, 0] = normed[:, :half]
        nbuf[m, 1] = normed[:, half:]
        exchange(gather_no, m, lambda other: nbuf.at[m, lax.rem(other, 2)], gbuf)

        @pl.when(m == 0)
        def _():
            weight_own().wait()
            weight_share().wait_recv()

        await_all(gather_no, m, gbuf)
        for k in range(0, half, step_k):
            part = gbuf[m, :, :, k : k + step_k].astype(F32).reshape(rows, step_k)
            xbuf[:, k : k + step_k] = part.astype(BF16)
        for c in range(0, chip_cols, 256):
            product = jnp.dot(xbuf[...], wbuf[:, c : c + 256], preferred_element_type=F32)
            pout[m, :, :, c : c + 256] = product.reshape(groups, seg_rows, 256).astype(BF16)
        exchange(part_no, m, lambda other: pout.at[m, other], pin)
        for copy in keep_copies(m):
            copy.start()
        await_all(part_no, m, pin)
        for q in range(chips):
            place = slice(q * chip_cols, (q + 1) * chip_cols)
            value = pin[m, 2 * q].astype(F32) + pin[m, 2 * q + 1].astype(F32)
            hidden[m, :, place] = value
            base = arrived_out[m, :, place].astype(F32)
            hop_out[m, :, place] = (base + gelu_value(value)).astype(BF16)

        @pl.when(jnp.logical_not(last))
        def _():
            hop(hop_no, m, hop_out, hop_in, after).start()

        return carry

    lax.fori_loop(0, micro, forward, 0)
    gain_sum[...] = jnp.zeros_like(gain_sum)

    def backward(m, carry):
        @pl.when(last)
        def _():
            up_in[m] = cotangent[m]

        @pl.when(jnp.logical_not(last))
        def _():
            hop(up_no, m, up_out, up_in, before).wait_recv()

        for q in range(chips):
            place = slice(q * chip_cols, (q + 1) * chip_cols)
            upstream = up_in[m, :, place].astype(F32)
            slopes[m, q] = (upstream * gelu_slope(hidden[m, :, place])).astype(BF16)
        exchange(slope_no, m, lambda other: slopes.at[m, lax.div(other, 2)], slope_in)
        await_all(slope_no, m, slope_in)
        ybuf[...] = slope_in[m].astype(F32).reshape(rows, chip_cols).astype(BF16)
        for k in range(0, half, step_k):
            product = lax.dot_general(
                ybuf[...],
                wbuf[k : k + step_k, :],
                (((1,), (1,)), ((), ())),
                preferred_element_type=F32,
            )
            back_out[m, :, :, k : k + step_k] = product.reshape(groups, seg_rows, step_k).astype(
                BF16
            )
        exchange(back_no, m, lambda other: back_out.at[m, other], back_in)
        slope_copy(m).start()
        await_all(back_no, m, back_in)
        halves = []
        for side in range(2):
            total = back_in[m, side].astype(F32)
            for q in range(1, chips):
                total = total + back_in[m, 2 * q + side].astype(F32)
            halves.append(total)
        back = jnp.concatenate(halves, axis=1)
        arrived_f = arrived_out[m].astype(F32)
        scale = scales[m][:, :1]
        gain_sum[...] += back * arrived_f * scale
        weighted = back * gains[...]
        mean_term = jnp.mean(weighted * arrived_f, axis=-1, keepdims=True)
        total = up_in[m].astype(F32) + scale * (weighted - arrived_f * scale * scale * mean_term)
        up_out[m] = total.astype(BF16)

        @pl.when(jnp.logical_not(first))
        def _():
            hop(up_no, m, up_out, up_in, before).start()

        return carry

    lax.fori_loop(0, micro, backward, 0)

    gain_row[...] = jnp.sum(gain_sum[...], axis=0, keepdims=True)
    gain_in[me] = gain_row[...]

    def gain_copy(other):
        return pltpu.make_async_remote_copy(
            src_ref=gain_row,
            dst_ref=gain_in.at[me],
            send_sem=gain_sem.at[0],
            recv_sem=gain_sem.at[1],
            device_id={"dp": other},
            device_id_type=MESH,
        )

    def gain_send(step, carry):
        gain_copy(lax.rem(me + step, groups)).start()
        return carry

    lax.fori_loop(1, groups, gain_send, 0)
    most = gain_in.at[pl.ds(0, groups - 1)]
    pltpu.make_async_copy(most, most, gain_sem.at[1]).wait()
    pltpu.make_async_copy(most, most, gain_sem.at[0]).wait()
    total = gain_in[0]
    for j in range(1, groups):
        total = total + gain_in[j]
    gain_out[...] = total

    weight_share().wait_send()

    def finish(m, carry):
        await_sent(gather_no, m, gbuf)
        await_sent(part_no, m, pin)
        await_sent(slope_no, m, slope_in)
        await_sent(back_no, m, back_in)
        shared, kept = keep_copies(m)
        shared.wait()
        kept.wait()
        slope_copy(m).wait()

        @pl.when(jnp.logical_not(last))
        def _():
            hop(hop_no, m, hop_out, hop_in, after).wait_send()

        @pl.when(jnp.logical_not(first))
        def _():
            hop(up_no, m, up_out, up_in, before).wait_send()

        return carry

    lax.fori_loop(0, micro, finish, 0)


def on_device(sections, groups, acts_in, weights, gains, stored, sample_ids, cotangent):
    micro, seg_rows, width = acts_in.shape
    own_cols = weights.shape[2]
    half = width // 2
    chip_cols = 2 * own_cols
    chips = groups // 2
    rows = groups * seg_rows
    vmem = pl.BlockSpec(memory_space=pltpu.VMEM)
    anywhere = pl.BlockSpec(memory_space=pl.ANY)
    smem = pl.BlockSpec(memory_space=pltpu.SMEM)
    arrived, normed, slope, gain = pl.pallas_call(
        functools.partial(relay, sections, groups),
        out_shape=(
            jax.ShapeDtypeStruct((micro, seg_rows, width), BF16),
            jax.ShapeDtypeStruct((2, micro, groups, seg_rows, half), BF16),
            jax.ShapeDtypeStruct((micro, groups, seg_rows, own_cols), BF16),
            jax.ShapeDtypeStruct((1, width), F32),
        ),
        in_specs=[smem, vmem, anywhere, vmem, vmem, vmem],
        out_specs=(vmem, anywhere, anywhere, vmem),
        scratch_shapes=[
            pltpu.VMEM((half, chip_cols), BF16),
            pltpu.VMEM((micro, 2, seg_rows, half), BF16),
            pltpu.VMEM((micro, groups, seg_rows, half), BF16),
            pltpu.VMEM((rows, half), BF16),
            pltpu.VMEM((micro, groups, seg_rows, chip_cols), BF16),
            pltpu.VMEM((micro, groups, seg_rows, chip_cols), BF16),
            pltpu.VMEM((micro, seg_rows, width), F32),
            pltpu.VMEM((micro, seg_rows, width), BF16),
            pltpu.VMEM((micro, seg_rows, width), BF16),
            pltpu.VMEM((micro, chips, seg_rows, chip_cols), BF16),
            pltpu.VMEM((micro, groups, seg_rows, chip_cols), BF16),
            pltpu.VMEM((rows, chip_cols), BF16),
            pltpu.VMEM((micro, groups, seg_rows, half), BF16),
            pltpu.VMEM((micro, groups, seg_rows, half), BF16),
            pltpu.VMEM((micro, seg_rows, width), BF16),
            pltpu.VMEM((micro, seg_rows, width), BF16),
            pltpu.VMEM((micro, seg_rows, 128), F32),
            pltpu.VMEM((seg_rows, width), F32),
            pltpu.VMEM((1, width), F32),
            pltpu.VMEM((groups, 1, width), F32),
            pltpu.SemaphoreType.DMA((3,)),
            pltpu.SemaphoreType.DMA((7, micro)),
            pltpu.SemaphoreType.DMA((7, micro)),
            pltpu.SemaphoreType.DMA((2, micro)),
            pltpu.SemaphoreType.DMA((2,)),
        ],
        compiler_params=pltpu.CompilerParams(
            collective_id=0, has_side_effects=True, vmem_limit_bytes=40 * 1024 * 1024
        ),
    )(sample_ids, acts_in, weights, gains, stored, cotangent)

    grad = lax.dot_general(
        normed.reshape(2, micro * rows, half),
        slope.reshape(micro * rows, own_cols),
        (((1,), (0,)), ((), ())),
        preferred_element_type=F32,
    ).reshape(1, width, own_cols)
    first_slot = lax.axis_index("dp") * stored.shape[1]
    kept = stored
    places = first_slot + jnp.arange(stored.shape[1], dtype=jnp.int32)
    for m in range(micro):
        here = (places == sample_ids[m, 0])[None, :, None, None]
        kept = jnp.where(here, arrived[m][None, None], kept)
    return (kept, grad, gain)


def solution(mesh):
    placed = (
        P(None, "dp", None),
        P("section", None, "dp"),
        P("section", None),
        P("section", "dp", None, None),
        P(None, "dp"),
        P(None, "dp", None),
    )
    return jax.shard_map(
        functools.partial(on_device, mesh.shape["section"], mesh.shape["dp"]),
        mesh=mesh,
        in_specs=placed,
        out_specs=(P("section", "dp", None, None), P("section", None, "dp"), P("section", None)),
        check_vma=False,
    )
```

```python
import functools

import jax
import jax.numpy as jnp
from jax import lax
from jax.experimental import pallas as pl
from jax.experimental.pallas import tpu as pltpu
from jax.sharding import PartitionSpec as P

MESH = pl.DeviceIdType.MESH
F32 = jnp.float32
BF16 = jnp.bfloat16

clip_limit = 1.0
epsilon = 1e-05
gelu_coeff = 0.7978845608028654


def gelu_value(values):
    inner = gelu_coeff * (values + 0.044715 * values * values * values)
    return 0.5 * values * (1.0 + jnp.tanh(inner))


def gelu_slope(values):
    tangent = jnp.tanh(gelu_coeff * (values + 0.044715 * values * values * values))
    return 0.5 * (1.0 + tangent) + 0.5 * values * (1.0 - tangent * tangent) * gelu_coeff * (
        1.0 + 0.134145 * values * values
    )


def relay(
    sections,
    groups,
    ids,
    acts_hbm,
    weights,
    gains_hbm,
    stored_hbm,
    cotangent_hbm,
    arrived_out,
    normed_out,
    slope_out,
    gain_out,
    acts,
    gains,
    stored,
    cotangent,
    wbuf,
    nbuf,
    gbuf,
    xbuf,
    pout,
    pin,
    hidden,
    incoming,
    arrived,
    arr_in,
    slopes,
    slope_in,
    ybuf,
    back_out,
    back_in,
    up_in,
    up_out,
    scales,
    gain_sum,
    gain_row,
    gain_part,
    gain_mine,
    gain_full,
    load_sem,
    w_sem,
    gather_send,
    gather_recv,
    part_send,
    part_recv,
    slope_send,
    slope_recv,
    back_send,
    back_recv,
    side_send,
    side_recv,
    keep_send,
    keep_recv,
    copy_sem,
    gain_sem,
):
    micro, seg_rows, width = acts.shape
    half = width // 2
    own_cols = weights.shape[2]
    chip_cols = 2 * own_cols
    chips = groups // 2
    rows = chips * seg_rows
    slot_count = stored.shape[1]
    section = lax.axis_index("section")
    me = lax.axis_index("dp")
    core = lax.rem(me, 2)
    chip = lax.div(me, 2)
    sibling = me + 1 - 2 * core
    first = section == 0
    last = section == sections - 1
    after = lax.rem(section + 1, sections)
    before = lax.rem(section + sections - 1, sections)
    step_k = 512

    loads = [
        pltpu.make_async_copy(source, target, load_sem.at[i])
        for i, (source, target) in enumerate(
            (
                (acts_hbm, acts),
                (stored_hbm, stored),
                (gains_hbm, gains),
                (cotangent_hbm, cotangent),
            )
        )
    ]
    for load in loads:
        load.start()
    own_place = pl.ds(pl.multiple_of(core * own_cols, 128), own_cols)
    weight_own = pltpu.make_async_copy(
        weights.at[0, pl.ds(core * half, half), :], wbuf.at[:, own_place], w_sem.at[2]
    )
    weight_own.start()

    barrier = pltpu.get_barrier_semaphore()

    def greet(step, carry):
        other = lax.rem(me + step, groups)
        for there in (after, before):
            pl.semaphore_signal(
                barrier, inc=1, device_id={"section": there, "dp": other}, device_id_type=MESH
            )

        @pl.when(step > 0)
        def _():
            pl.semaphore_signal(
                barrier, inc=1, device_id={"section": section, "dp": other}, device_id_type=MESH
            )

        return carry

    lax.fori_loop(0, groups, greet, 0)
    pl.semaphore_wait(barrier, 3 * groups - 1)

    weight_share = pltpu.make_async_remote_copy(
        src_ref=weights.at[0, pl.ds((1 - core) * half, half), :],
        dst_ref=wbuf.at[:, own_place],
        send_sem=w_sem.at[0],
        recv_sem=w_sem.at[1],
        device_id={"dp": sibling},
        device_id_type=MESH,
    )
    weight_share.start()
    loads[0].wait()
    loads[1].wait()
    loads[2].wait()
    loads[3].wait()
    gain_sum[...] = jnp.zeros_like(gain_sum)

    def remote(source, target, send, recv, there, other):
        return pltpu.make_async_remote_copy(
            src_ref=source,
            dst_ref=target,
            send_sem=send,
            recv_sem=recv,
            device_id={"section": there, "dp": other},
            device_id_type=MESH,
        )

    def await_bytes(ref, sem):
        pltpu.make_async_copy(ref, ref, sem).wait()

    def keep_place(m, chain):
        return pl.ds(pl.multiple_of((m * 2 + chain) * rows, rows), rows)

    def keep_share(m, chain):
        return remote(
            xbuf.at[m, chain],
            normed_out.at[core, keep_place(m, chain), :],
            keep_send.at[m, chain],
            keep_recv.at[m, chain],
            section,
            sibling,
        )

    def keep_own(m, chain):
        return pltpu.make_async_copy(
            xbuf.at[m, chain],
            normed_out.at[core, keep_place(m, chain), :],
            copy_sem.at[0, m, chain],
        )

    def slope_copy(m, chain):
        return pltpu.make_async_copy(
            ybuf.at[m, chain, :, own_place],
            slope_out.at[keep_place(m, chain), :],
            copy_sem.at[1, m, chain],
        )

    def send_slopes(kind, m, there, remote_own):
        def send(step, carry):
            other = lax.rem(me + step, groups)
            remote(
                slopes.at[kind, m, lax.div(other, 2)],
                slope_in.at[m, core, chip],
                slope_send.at[kind, m],
                slope_recv.at[m, core],
                there,
                other,
            ).start()
            return carry

        if remote_own:
            lax.fori_loop(0, groups, send, 0)
        else:
            lax.fori_loop(1, groups, send, 0)
            pltpu.make_async_copy(
                slopes.at[kind, m, chip], slope_in.at[m, core, chip], slope_recv.at[m, core]
            ).start()

    def part(q):
        return slice(q * chip_cols, (q + 1) * chip_cols)

    def summed_parts(kind, m, q):
        return pin[kind, m, 2 * q].astype(F32) + pin[kind, m, 2 * q + 1].astype(F32)

    def forward_rows(m):
        @pl.when(first)
        def _():
            incoming[...] = acts[m].astype(F32)

        @pl.when(jnp.logical_not(first))
        def _():
            await_bytes(arr_in.at[m], side_recv.at[0, m])
            await_bytes(pin.at[0, m], part_recv.at[0, m])
            for q in range(chips):
                value = summed_parts(0, m, q)
                hidden[m, :, part(q)] = value
                total = arr_in[m, :, part(q)].astype(F32) + gelu_value(value)
                incoming[:, part(q)] = total.astype(BF16).astype(F32)

        slot = jnp.clip(ids[m, 0] - me * slot_count, 0, slot_count - 1)
        previous = stored[0, slot].astype(F32)
        moved = jnp.clip(incoming[...] - previous, -clip_limit, clip_limit)
        arrived_now = (previous + moved).astype(BF16)
        arrived[m] = arrived_now
        arrived_f = arrived_now.astype(F32)
        scale = lax.rsqrt(jnp.mean(arrived_f * arrived_f, axis=-1, keepdims=True) + epsilon)
        scales[m] = jnp.broadcast_to(scale, (seg_rows, 128))
        normed = (arrived_f * scale * gains[...]).astype(BF16)
        nbuf[m, 0] = normed[:, :half]
        nbuf[m, 1] = normed[:, half:]

        def send(step, carry):
            other = lax.rem(me + step, groups)
            remote(
                nbuf.at[m, lax.rem(other, 2)],
                gbuf.at[m, core, chip],
                gather_send.at[m],
                gather_recv.at[m, core],
                section,
                other,
            ).start()
            return carry

        lax.fori_loop(1, groups, send, 0)
        pltpu.make_async_copy(
            nbuf.at[m, core], gbuf.at[m, core, chip], gather_recv.at[m, core]
        ).start()

        @pl.when(jnp.logical_not(last))
        def _():
            remote(
                arrived.at[m], arr_in.at[m], side_send.at[0, m], side_recv.at[0, m], after, me
            ).start()

        @pl.when(jnp.logical_not(first))
        def _():
            for q in range(chips):
                hidden[m, :, part(q)] = gelu_slope(hidden[m, :, part(q)])

    def forward_columns(m, chain):
        @pl.when((m == 0) & (chain == 0))
        def _():
            weight_own.wait()
            weight_share.wait_recv()

        await_bytes(gbuf.at[m, chain], gather_recv.at[m, chain])
        for k in range(0, half, step_k):
            piece = gbuf[m, chain, :, :, k : k + step_k].astype(F32).reshape(rows, step_k)
            xbuf[m, chain, :, k : k + step_k] = piece.astype(BF16)
        for c in range(0, chip_cols, 256):
            product = jnp.dot(
                xbuf[m, chain], wbuf[:, c : c + 256], preferred_element_type=F32
            )
            pout[m, chain, :, :, c : c + 256] = product.reshape(chips, seg_rows, 256).astype(BF16)

        def send(step, carry):
            q = lax.rem(chip + step, chips)
            other = 2 * q + chain

            @pl.when(jnp.logical_not(last))
            def _():
                remote(
                    pout.at[m, chain, q],
                    pin.at[0, m, me],
                    part_send.at[m, chain],
                    part_recv.at[0, m],
                    after,
                    other,
                ).start()

            @pl.when(last & (other != me))
            def _():
                remote(
                    pout.at[m, chain, q],
                    pin.at[1, m, me],
                    part_send.at[m, chain],
                    part_recv.at[1, m],
                    section,
                    other,
                ).start()

            return carry

        lax.fori_loop(0, chips, send, 0)

        @pl.when(last & (core == chain))
        def _():
            pltpu.make_async_copy(
                pout.at[m, chain, chip], pin.at[1, m, me], part_recv.at[1, m]
            ).start()

        keep_share(m, chain).start()
        keep_own(m, chain).start()

    def turn_rows(m):
        await_bytes(pin.at[1, m], part_recv.at[1, m])
        for q in range(chips):
            slope = cotangent[m, :, part(q)].astype(F32) * gelu_slope(summed_parts(1, m, q))
            slopes[1, m, q] = slope.astype(BF16)
        send_slopes(1, m, section, False)

    def backward_columns(m, chain):
        await_bytes(slope_in.at[m, chain], slope_recv.at[m, chain])
        ybuf[m, chain] = slope_in[m, chain].astype(F32).reshape(rows, chip_cols).astype(BF16)
        for k in range(0, half, step_k):
            product = lax.dot_general(
                ybuf[m, chain],
                wbuf[k : k + step_k, :],
                (((1,), (1,)), ((), ())),
                preferred_element_type=F32,
            )
            shaped = product.reshape(chips, seg_rows, step_k).astype(BF16)
            back_out[m, chain, :, :, k : k + step_k] = shaped

        def send(step, carry):
            q = lax.rem(chip + step, chips)
            other = 2 * q + chain

            @pl.when(other != me)
            def _():
                remote(
                    back_out.at[m, chain, q],
                    back_in.at[m, me],
                    back_send.at[m, chain],
                    back_recv.at[m],
                    section,
                    other,
                ).start()

            return carry

        lax.fori_loop(0, chips, send, 0)

        @pl.when(core == chain)
        def _():
            pltpu.make_async_copy(
                back_out.at[m, chain, chip], back_in.at[m, me], back_recv.at[m]
            ).start()

        slope_copy(m, chain).start()

    def backward_rows(m):
        @pl.when(last)
        def _():
            up_in[m] = cotangent[m]

        @pl.when(jnp.logical_not(last))
        def _():
            await_bytes(up_in.at[m], side_recv.at[1, m])

        await_bytes(back_in.at[m], back_recv.at[m])
        halves = []
        for side in range(2):
            total = back_in[m, side].astype(F32)
            for q in range(1, chips):
                total = total + back_in[m, 2 * q + side].astype(F32)
            halves.append(total)
        back = jnp.concatenate(halves, axis=1)
        arrived_f = arrived[m].astype(F32)
        scale = scales[m][:, :1]
        gain_sum[...] += back * arrived_f * scale

        @pl.when(jnp.logical_not(first))
        def _():
            weighted = back * gains[...]
            mean_term = jnp.mean(weighted * arrived_f, axis=-1, keepdims=True)
            total = up_in[m].astype(F32) + scale * (
                weighted - arrived_f * scale * scale * mean_term
            )
            up_out[m] = total.astype(BF16)
            for q in range(chips):
                slope = up_out[m, :, part(q)].astype(F32) * hidden[m, :, part(q)]
                slopes[0, m, q] = slope.astype(BF16)
            send_slopes(0, m, before, True)
            remote(
                up_out.at[m], up_in.at[m], side_send.at[1, m], side_recv.at[1, m], before, me
            ).start()

    FR, FC, TR, BC, BR, NO = range(6)

    def code(kind, m=0, chain=0):
        return kind * 4 + m * 2 + chain

    plain = [
        [(FR, 0), (FC, 0, 0), (FC, 0, 1), (FR, 1), (FC, 1, 0), (FC, 1, 1),
         (BC, 0, 0), (BR, 0), (BC, 0, 1), (BC, 1, 0), (BR, 1), (BC, 1, 1)],
        [(FC, 0, 0), (FR, 0), (FC, 0, 1), (FC, 1, 0), (FR, 1), (FC, 1, 1),
         (BC, 0, 0), (BC, 0, 1), (BR, 0), (BC, 1, 0), (BC, 1, 1), (BR, 1)],
    ]
    turning = [
        [(FR, 0), (FC, 0, 0), (TR, 0), (FC, 0, 1), (FR, 1), (BC, 0, 0), (FC, 1, 0),
         (BC, 0, 1), (BR, 0), (TR, 1), (FC, 1, 1), (BC, 1, 0), (BR, 1), (BC, 1, 1)],
        [(FC, 0, 0), (FR, 0), (FC, 0, 1), (BC, 0, 0), (TR, 0), (FC, 1, 0), (FR, 1),
         (BC, 0, 1), (FC, 1, 1), (BC, 1, 0), (BR, 0), (TR, 1), (BC, 1, 1), (BR, 1)],
    ]
    orders = [
        [[code(*entry) for entry in order + [(NO,)] * (14 - len(order))] for order in pair]
        for pair in (plain, turning)
    ]

    def run(t, carry):
        def chosen(order):
            value = order[0]
            for i in range(1, len(order)):
                value = jnp.where(t == i, order[i], value)
            return value

        now = jnp.where(
            last,
            jnp.where(core == 0, chosen(orders[1][0]), chosen(orders[1][1])),
            jnp.where(core == 0, chosen(orders[0][0]), chosen(orders[0][1])),
        )
        kind = lax.div(now, 4)
        m = lax.rem(lax.div(now, 2), 2)
        chain = lax.rem(now, 2)
        pl.when(kind == FR)(lambda: forward_rows(m))
        pl.when(kind == FC)(lambda: forward_columns(m, chain))
        pl.when(kind == TR)(lambda: turn_rows(m))
        pl.when(kind == BC)(lambda: backward_columns(m, chain))
        pl.when(kind == BR)(lambda: backward_rows(m))
        return carry

    lax.fori_loop(0, 14, run, 0)

    gain_row[...] = jnp.sum(gain_sum[...], axis=0, keepdims=True)

    def gain_place(other):
        return pl.ds(pl.multiple_of(other * own_cols, 128), own_cols)

    def gain_scatter(step, carry):
        other = lax.rem(me + step, groups)
        remote(
            gain_row.at[:, gain_place(other)],
            gain_part.at[me],
            gain_sem.at[0],
            gain_sem.at[1],
            section,
            other,
        ).start()
        return carry

    lax.fori_loop(1, groups, gain_scatter, 0)
    pltpu.make_async_copy(
        gain_row.at[:, gain_place(me)], gain_part.at[me], gain_sem.at[1]
    ).start()
    await_bytes(gain_part, gain_sem.at[1])
    total = gain_part[0]
    for j in range(1, groups):
        total = total + gain_part[j]
    gain_mine[...] = total

    def gain_spread(step, carry):
        other = lax.rem(me + step, groups)
        remote(
            gain_mine,
            gain_full.at[:, gain_place(me)],
            gain_sem.at[2],
            gain_sem.at[3],
            section,
            other,
        ).start()
        return carry

    lax.fori_loop(1, groups, gain_spread, 0)
    pltpu.make_async_copy(gain_mine, gain_full.at[:, gain_place(me)], gain_sem.at[3]).start()

    arrived_copy = pltpu.make_async_copy(arrived, arrived_out, gain_sem.at[4])
    arrived_copy.start()
    weight_share.wait_send()
    for m in range(micro):
        await_bytes(back_in.at[m, 0 : groups - 1], gather_send.at[m])
        for chain in range(2):

            @pl.when(last & (core == chain))
            def _(m=m, chain=chain):
                await_bytes(pout.at[m, chain, 0 : chips - 1], part_send.at[m, chain])

            @pl.when(jnp.logical_not(last & (core == chain)))
            def _(m=m, chain=chain):
                await_bytes(pout.at[m, chain], part_send.at[m, chain])

            @pl.when(core == chain)
            def _(m=m, chain=chain):
                await_bytes(back_out.at[m, chain, 0 : chips - 1], back_send.at[m, chain])

            @pl.when(core != chain)
            def _(m=m, chain=chain):
                await_bytes(back_out.at[m, chain], back_send.at[m, chain])

            keep_share(m, chain).wait()
            keep_own(m, chain).wait()
            slope_copy(m, chain).wait()

        @pl.when(last)
        def _(m=m):
            await_bytes(pin.at[1, m, 0 : groups - 1], slope_send.at[1, m])

        @pl.when(jnp.logical_not(first))
        def _(m=m):
            await_bytes(pin.at[0, m], slope_send.at[0, m])
            await_bytes(up_out.at[m], side_send.at[1, m])

        @pl.when(jnp.logical_not(last))
        def _(m=m):
            await_bytes(arrived.at[m], side_send.at[0, m])

    most = gain_part.at[0 : groups - 1]
    await_bytes(most, gain_sem.at[0])
    await_bytes(gain_full, gain_sem.at[3])
    await_bytes(most, gain_sem.at[2])
    gain_copy = pltpu.make_async_copy(gain_full, gain_out, gain_sem.at[5])
    gain_copy.start()
    arrived_copy.wait()
    gain_copy.wait()


def on_device(sections, groups, acts_in, weights, gains, stored, sample_ids, cotangent):
    micro, seg_rows, width = acts_in.shape
    own_cols = weights.shape[2]
    half = width // 2
    chip_cols = 2 * own_cols
    chips = groups // 2
    rows = chips * seg_rows
    anywhere = pl.BlockSpec(memory_space=pl.ANY)
    smem = pl.BlockSpec(memory_space=pltpu.SMEM)
    dma = pltpu.SemaphoreType.DMA
    arrived, normed, slope, gain = pl.pallas_call(
        functools.partial(relay, sections, groups),
        out_shape=(
            jax.ShapeDtypeStruct((micro, seg_rows, width), BF16),
            jax.ShapeDtypeStruct((2, micro * 2 * rows, half), BF16),
            jax.ShapeDtypeStruct((micro * 2 * rows, own_cols), BF16),
            jax.ShapeDtypeStruct((1, width), F32),
        ),
        in_specs=[smem] + [anywhere] * 5,
        out_specs=(anywhere,) * 4,
        scratch_shapes=[
            pltpu.VMEM((micro, seg_rows, width), BF16),
            pltpu.VMEM((1, width), F32),
            pltpu.VMEM(stored.shape, BF16),
            pltpu.VMEM((micro, seg_rows, width), BF16),
            pltpu.VMEM((half, chip_cols), BF16),
            pltpu.VMEM((micro, 2, seg_rows, half), BF16),
            pltpu.VMEM((micro, 2, chips, seg_rows, half), BF16),
            pltpu.VMEM((micro, 2, rows, half), BF16),
            pltpu.VMEM((micro, 2, chips, seg_rows, chip_cols), BF16),
            pltpu.VMEM((2, micro, groups, seg_rows, chip_cols), BF16),
            pltpu.VMEM((micro, seg_rows, width), F32),
            pltpu.VMEM((seg_rows, width), F32),
            pltpu.VMEM((micro, seg_rows, width), BF16),
            pltpu.VMEM((micro, seg_rows, width), BF16),
            pltpu.VMEM((2, micro, chips, seg_rows, chip_cols), BF16),
            pltpu.VMEM((micro, 2, chips, seg_rows, chip_cols), BF16),
            pltpu.VMEM((micro, 2, rows, chip_cols), BF16),
            pltpu.VMEM((micro, 2, chips, seg_rows, half), BF16),
            pltpu.VMEM((micro, groups, seg_rows, half), BF16),
            pltpu.VMEM((micro, seg_rows, width), BF16),
            pltpu.VMEM((micro, seg_rows, width), BF16),
            pltpu.VMEM((micro, seg_rows, 128), F32),
            pltpu.VMEM((seg_rows, width), F32),
            pltpu.VMEM((1, width), F32),
            pltpu.VMEM((groups, 1, own_cols), F32),
            pltpu.VMEM((1, own_cols), F32),
            pltpu.VMEM((1, width), F32),
            dma((4,)),
            dma((3,)),
            dma((micro,)),
            dma((micro, 2)),
            dma((micro, 2)),
            dma((2, micro)),
            dma((2, micro)),
            dma((micro, 2)),
            dma((micro, 2)),
            dma((micro,)),
            dma((2, micro)),
            dma((2, micro)),
            dma((micro, 2)),
            dma((micro, 2)),
            dma((2, micro, 2)),
            dma((6,)),
        ],
        compiler_params=pltpu.CompilerParams(
            collective_id=0, has_side_effects=True, vmem_limit_bytes=48 * 1024 * 1024
        ),
    )(sample_ids, acts_in, weights, gains, stored, cotangent)

    block_k = 768
    blocks = half // block_k

    def grad_block(normed_ref, slope_ref, grad_ref):
        grad_ref[0] = lax.dot_general(
            normed_ref[0],
            slope_ref[...],
            (((0,), (0,)), ((), ())),
            preferred_element_type=F32,
        )

    grad = pl.pallas_call(
        grad_block,
        grid=(2 * blocks,),
        out_shape=jax.ShapeDtypeStruct((1, width, own_cols), F32),
        in_specs=[
            pl.BlockSpec((1, micro * 2 * rows, block_k), lambda i: (i // blocks, 0, i % blocks)),
            pl.BlockSpec((micro * 2 * rows, own_cols), lambda i: (0, 0)),
        ],
        out_specs=pl.BlockSpec((1, block_k, own_cols), lambda i: (0, i, 0)),
    )(normed, slope)

    slot_count = stored.shape[1]
    places = lax.axis_index("dp") * slot_count + jnp.arange(slot_count, dtype=jnp.int32)
    kept = stored
    for m in range(micro):
        here = (places == sample_ids[m, 0])[None, :, None, None]
        kept = jnp.where(here, arrived[m][None, None], kept)
    return (kept, grad, gain)


def solution(mesh):
    placed = (
        P(None, "dp", None),
        P("section", None, "dp"),
        P("section", None),
        P("section", "dp", None, None),
        P(None, "dp"),
        P(None, "dp", None),
    )
    return jax.shard_map(
        functools.partial(on_device, mesh.shape["section"], mesh.shape["dp"]),
        mesh=mesh,
        in_specs=placed,
        out_specs=(P("section", "dp", None, None), P("section", None, "dp"), P("section", None)),
        check_vma=False,
    )
```

```python
import functools

import jax
import jax.numpy as jnp
from jax import lax
from jax.experimental import pallas as pl
from jax.experimental.pallas import tpu as pltpu
from jax.sharding import PartitionSpec as P

MESH = pl.DeviceIdType.MESH
F32 = jnp.float32
BF16 = jnp.bfloat16

clip_limit = 1.0
epsilon = 1e-05
gelu_coeff = 0.7978845608028654


def gelu_value(values):
    inner = gelu_coeff * (values + 0.044715 * values * values * values)
    return 0.5 * values * (1.0 + jnp.tanh(inner))


def gelu_slope(values):
    tangent = jnp.tanh(gelu_coeff * (values + 0.044715 * values * values * values))
    return 0.5 * (1.0 + tangent) + 0.5 * values * (1.0 - tangent * tangent) * gelu_coeff * (
        1.0 + 0.134145 * values * values
    )


def relay(
    sections,
    groups,
    ids,
    acts_hbm,
    weights,
    gains_hbm,
    stored_hbm,
    cotangent_hbm,
    arrived_out,
    normed_out,
    slope_out,
    gain_out,
    acts,
    gains,
    stored,
    cotangent,
    wbuf,
    nbuf,
    gbuf,
    xbuf,
    pout,
    pin,
    hidden,
    incoming,
    arrived,
    arr_in,
    slopes,
    slope_in,
    ybuf,
    back_out,
    back_in,
    up_in,
    up_out,
    scales,
    xturned,
    partial_sum,
    gain_sum,
    gain_row,
    gain_in,
    gain_full,
    load_sem,
    w_sem,
    gather_send,
    gather_recv,
    part_send,
    part_recv,
    slope_send,
    slope_recv,
    back_send,
    back_recv,
    side_send,
    side_recv,
    keep_send,
    keep_recv,
    copy_sem,
    gain_sem,
):
    micro, seg_rows, width = acts.shape
    half = width // 2
    own_cols = weights.shape[2]
    chip_cols = 2 * own_cols
    chips = groups // 2
    rows = chips * seg_rows
    slot_count = stored.shape[1]
    section = lax.axis_index("section")
    me = lax.axis_index("dp")
    core = lax.rem(me, 2)
    chip = lax.div(me, 2)
    sibling = me + 1 - 2 * core
    first = section == 0
    last = section == sections - 1
    after = lax.rem(section + 1, sections)
    before = lax.rem(section + sections - 1, sections)
    step_k = 1024
    parts = 3
    span = half // parts
    z_count = groups // 4
    z_pos = lax.div(me, 4)
    x_pos = lax.rem(chip, 2)

    loads = [
        pltpu.make_async_copy(source, target, load_sem.at[i])
        for i, (source, target) in enumerate(
            (
                (acts_hbm, acts),
                (stored_hbm, stored),
                (gains_hbm, gains),
                (cotangent_hbm, cotangent),
            )
        )
    ]
    for load in loads:
        load.start()
    own_place = pl.ds(pl.multiple_of(core * own_cols, 128), own_cols)
    weight_own = pltpu.make_async_copy(
        weights.at[0, pl.ds(core * half, half), :], wbuf.at[:, own_place], w_sem.at[2]
    )
    weight_own.start()

    barrier = pltpu.get_barrier_semaphore()

    def greet(step, carry):
        other = lax.rem(me + step, groups)
        for there in (after, before):
            pl.semaphore_signal(
                barrier, inc=1, device_id={"section": there, "dp": other}, device_id_type=MESH
            )

        @pl.when(step > 0)
        def _():
            pl.semaphore_signal(
                barrier, inc=1, device_id={"section": section, "dp": other}, device_id_type=MESH
            )

        return carry

    lax.fori_loop(0, groups, greet, 0)
    pl.semaphore_wait(barrier, 3 * groups - 1)

    weight_share = pltpu.make_async_remote_copy(
        src_ref=weights.at[0, pl.ds((1 - core) * half, half), :],
        dst_ref=wbuf.at[:, own_place],
        send_sem=w_sem.at[0],
        recv_sem=w_sem.at[1],
        device_id={"dp": sibling},
        device_id_type=MESH,
    )
    weight_share.start()
    loads[0].wait()
    loads[1].wait()
    loads[2].wait()
    loads[3].wait()
    gain_sum[...] = jnp.zeros_like(gain_sum)

    def remote(source, target, send, recv, there, other):
        return pltpu.make_async_remote_copy(
            src_ref=source,
            dst_ref=target,
            send_sem=send,
            recv_sem=recv,
            device_id={"section": there, "dp": other},
            device_id_type=MESH,
        )

    def far_z(i):
        away = jnp.where(i == 3, 0, jnp.where(i == 0, 2, 2 * i - 1))
        return lax.rem(z_pos + away, z_count)

    def far_device(i):
        x = lax.rem(x_pos + 1 - lax.rem(lax.div(i, 2), 2), 2)
        return far_z(lax.div(i, 4)) * 4 + x * 2 + lax.rem(core + 1 - lax.rem(i, 2), 2)

    def far_chip(i):
        return far_z(lax.div(i, 2)) * 2 + lax.rem(x_pos + 1 - lax.rem(i, 2), 2)

    def await_bytes(ref, sem):
        pltpu.make_async_copy(ref, ref, sem).wait()

    def keep_place(m, chain):
        return pl.ds(pl.multiple_of((m * 2 + chain) * rows, rows), rows)

    def turned_place(m):
        wide = 2 * rows
        return (
            pl.ds(pl.multiple_of(core * half, half), half),
            pl.ds(pl.multiple_of(m * wide, wide), wide),
        )

    def keep_share(m):
        return remote(
            xturned.at[m],
            normed_out.at[turned_place(m)],
            keep_send.at[m],
            keep_recv.at[m],
            section,
            sibling,
        )

    def keep_own(m):
        return pltpu.make_async_copy(
            xturned.at[m], normed_out.at[turned_place(m)], copy_sem.at[0, m, 0]
        )

    def turn_normed(m):
        for k in range(0, half, step_k):
            piece = xbuf[m, :, :, k : k + step_k].reshape(2 * rows, step_k).astype(F32)
            xturned[m, k : k + step_k, :] = jnp.transpose(piece).astype(BF16)
        keep_share(m).start()
        keep_own(m).start()

    def slope_copy(m, chain):
        return pltpu.make_async_copy(
            ybuf.at[m, chain, :, own_place],
            slope_out.at[keep_place(m, chain), :],
            copy_sem.at[1, m, chain],
        )

    def send_slopes(kind, m, there, remote_own):
        def send(step, carry):
            other = far_device(step)
            remote(
                slopes.at[kind, m, lax.div(other, 2)],
                slope_in.at[m, core, chip],
                slope_send.at[kind, m],
                slope_recv.at[m, core],
                there,
                other,
            ).start()
            return carry

        if remote_own:
            lax.fori_loop(0, groups, send, 0)
        else:
            lax.fori_loop(0, groups - 1, send, 0)
            pltpu.make_async_copy(
                slopes.at[kind, m, chip], slope_in.at[m, core, chip], slope_recv.at[m, core]
            ).start()

    def part(q):
        return slice(q * chip_cols, (q + 1) * chip_cols)

    def summed_parts(kind, m, q):
        return pin[kind, m, 2 * q].astype(F32) + pin[kind, m, 2 * q + 1].astype(F32)

    def forward_rows(m):
        @pl.when(first)
        def _():
            incoming[...] = acts[m].astype(F32)

        @pl.when(jnp.logical_not(first))
        def _():
            await_bytes(arr_in.at[m], side_recv.at[0, m])
            await_bytes(pin.at[0, m], part_recv.at[0, m])
            for q in range(chips):
                value = summed_parts(0, m, q)
                hidden[m, :, part(q)] = value
                total = arr_in[m, :, part(q)].astype(F32) + gelu_value(value)
                incoming[:, part(q)] = total.astype(BF16).astype(F32)

        slot = jnp.clip(ids[m, 0] - me * slot_count, 0, slot_count - 1)
        previous = stored[0, slot].astype(F32)
        moved = jnp.clip(incoming[...] - previous, -clip_limit, clip_limit)
        arrived_now = (previous + moved).astype(BF16)
        arrived[m] = arrived_now
        arrived_f = arrived_now.astype(F32)
        scale = lax.rsqrt(jnp.mean(arrived_f * arrived_f, axis=-1, keepdims=True) + epsilon)
        scales[m] = jnp.broadcast_to(scale, (seg_rows, 128))
        normed = (arrived_f * scale * gains[...]).astype(BF16)
        for side in range(2):
            for p in range(parts):
                start = side * half + p * span
                nbuf[m, p, side] = normed[:, start : start + span]
        for p in range(parts):

            def send(step, carry, p=p):
                other = far_device(step)
                remote(
                    nbuf.at[m, p, lax.rem(other, 2)],
                    gbuf.at[m, core, p, chip],
                    gather_send.at[m],
                    gather_recv.at[m, core, p],
                    section,
                    other,
                ).start()
                return carry

            lax.fori_loop(0, groups - 1, send, 0)
            pltpu.make_async_copy(
                nbuf.at[m, p, core], gbuf.at[m, core, p, chip], gather_recv.at[m, core, p]
            ).start()

        @pl.when(jnp.logical_not(last))
        def _():
            remote(
                arrived.at[m], arr_in.at[m], side_send.at[0, m], side_recv.at[0, m], after, me
            ).start()

        @pl.when(jnp.logical_not(first))
        def _():
            for q in range(chips):
                hidden[m, :, part(q)] = gelu_slope(hidden[m, :, part(q)])

    def forward_columns(m, chain):
        @pl.when((m == 0) & (chain == 0))
        def _():
            weight_own.wait()
            weight_share.wait_recv()

        for p in range(parts):
            await_bytes(gbuf.at[m, chain, p], gather_recv.at[m, chain, p])
            base = p * span
            for k in range(0, span, step_k):
                piece = gbuf[m, chain, p, :, :, k : k + step_k].astype(F32).reshape(rows, step_k)
                xbuf[m, chain, :, base + k : base + k + step_k] = piece.astype(BF16)
            for c in range(0, chip_cols, 256):
                product = jnp.dot(
                    xbuf[m, chain, :, base : base + span],
                    wbuf[base : base + span, c : c + 256],
                    preferred_element_type=F32,
                )
                if p > 0:
                    product = product + partial_sum[:, c : c + 256]
                if p + 1 < parts:
                    partial_sum[:, c : c + 256] = product
                else:
                    shaped = product.reshape(chips, seg_rows, 256).astype(BF16)
                    pout[m, chain, :, :, c : c + 256] = shaped

        def send(step, carry):
            q = far_chip(step)
            other = 2 * q + chain

            @pl.when(jnp.logical_not(last))
            def _():
                remote(
                    pout.at[m, chain, q],
                    pin.at[0, m, me],
                    part_send.at[m, chain],
                    part_recv.at[0, m],
                    after,
                    other,
                ).start()

            @pl.when(last & (other != me))
            def _():
                remote(
                    pout.at[m, chain, q],
                    pin.at[1, m, me],
                    part_send.at[m, chain],
                    part_recv.at[1, m],
                    section,
                    other,
                ).start()

            return carry

        lax.fori_loop(0, chips, send, 0)

        @pl.when(last & (core == chain))
        def _():
            pltpu.make_async_copy(
                pout.at[m, chain, chip], pin.at[1, m, me], part_recv.at[1, m]
            ).start()

    def turn_rows(m):
        await_bytes(pin.at[1, m], part_recv.at[1, m])
        for q in range(chips):
            slope = cotangent[m, :, part(q)].astype(F32) * gelu_slope(summed_parts(1, m, q))
            slopes[1, m, q] = slope.astype(BF16)
        send_slopes(1, m, section, False)

    def backward_columns(m, chain):
        await_bytes(slope_in.at[m, chain], slope_recv.at[m, chain])
        ybuf[m, chain] = slope_in[m, chain].astype(F32).reshape(rows, chip_cols).astype(BF16)
        for p in range(parts):
            for k in range(0, span, step_k):
                product = lax.dot_general(
                    ybuf[m, chain],
                    wbuf[p * span + k : p * span + k + step_k, :],
                    (((1,), (1,)), ((), ())),
                    preferred_element_type=F32,
                )
                shaped = product.reshape(chips, seg_rows, step_k).astype(BF16)
                back_out[m, chain, p, :, :, k : k + step_k] = shaped

            def send(step, carry, p=p):
                q = far_chip(step)
                other = 2 * q + chain

                @pl.when(other != me)
                def _():
                    remote(
                        back_out.at[m, chain, p, q],
                        back_in.at[m, p, me],
                        back_send.at[m, chain],
                        back_recv.at[m],
                        section,
                        other,
                    ).start()

                return carry

            @pl.when(jnp.logical_not(first))
            def _(p=p, send=send):
                lax.fori_loop(0, chips, send, 0)

            @pl.when(jnp.logical_not(first) & (core == chain))
            def _(p=p):
                pltpu.make_async_copy(
                    back_out.at[m, chain, p, chip], back_in.at[m, p, me], back_recv.at[m]
                ).start()

        for p in range(parts):
            for k in range(0, span, step_k):
                term = back_out[m, chain, p, :, :, k : k + step_k].astype(F32) * gbuf[
                    m, chain, p, :, :, k : k + step_k
                ].astype(F32)
                place = slice(p * span + k, p * span + k + step_k)
                gain_sum[:, place] += jnp.sum(term, axis=0)
        slope_copy(m, chain).start()

    def backward_rows(m):
        @pl.when(last)
        def _():
            up_in[m] = cotangent[m]

        @pl.when(jnp.logical_not(last))
        def _():
            await_bytes(up_in.at[m], side_recv.at[1, m])

        await_bytes(back_in.at[m], back_recv.at[m])
        pieces = []
        for side in range(2):
            for p in range(parts):
                total = back_in[m, p, side].astype(F32)
                for q in range(1, chips):
                    total = total + back_in[m, p, 2 * q + side].astype(F32)
                pieces.append(total)
        back = jnp.concatenate(pieces, axis=1)
        arrived_f = arrived[m].astype(F32)
        scale = scales[m][:, :1]
        weighted = back * gains[...]
        mean_term = jnp.mean(weighted * arrived_f, axis=-1, keepdims=True)
        total = up_in[m].astype(F32) + scale * (weighted - arrived_f * scale * scale * mean_term)
        up_out[m] = total.astype(BF16)
        for q in range(chips):
            slope = up_out[m, :, part(q)].astype(F32) * hidden[m, :, part(q)]
            slopes[0, m, q] = slope.astype(BF16)
        send_slopes(0, m, before, True)

        @pl.when(section > 1)
        def _():
            remote(
                up_out.at[m], up_in.at[m], side_send.at[1, m], side_recv.at[1, m], before, me
            ).start()

    FR, FC, TR, BC, BR, TN, NO = range(7)

    def code(kind, m=0, chain=0):
        return kind * 4 + m * 2 + chain

    plain = [
        [(FR, 0), (FC, 0, 0), (FC, 0, 1), (FR, 1), (FC, 1, 0), (FC, 1, 1),
         (TN, 0), (TN, 1), (BC, 0, 0), (BR, 0), (BC, 0, 1), (BC, 1, 0), (BR, 1), (BC, 1, 1)],
        [(FC, 0, 0), (FR, 0), (FC, 0, 1), (FC, 1, 0), (FR, 1), (FC, 1, 1),
         (TN, 0), (TN, 1), (BC, 0, 0), (BC, 0, 1), (BR, 0), (BC, 1, 0), (BC, 1, 1), (BR, 1)],
    ]
    turning = [
        [(FR, 0), (FC, 0, 0), (TR, 0), (FC, 0, 1), (FR, 1), (BC, 0, 0), (FC, 1, 0),
         (BC, 0, 1), (BR, 0), (TR, 1), (FC, 1, 1), (BC, 1, 0), (BR, 1), (BC, 1, 1), (TN, 0), (TN, 1)],
        [(FC, 0, 0), (FR, 0), (FC, 0, 1), (BC, 0, 0), (TR, 0), (FC, 1, 0), (FR, 1),
         (BC, 0, 1), (FC, 1, 1), (BC, 1, 0), (BR, 0), (TR, 1), (BC, 1, 1), (BR, 1), (TN, 0), (TN, 1)],
    ]
    orders = [
        [[code(*entry) for entry in order + [(NO,)] * (16 - len(order))] for order in pair]
        for pair in (plain, turning)
    ]

    def run(t, carry):
        def chosen(order):
            value = order[0]
            for i in range(1, len(order)):
                value = jnp.where(t == i, order[i], value)
            return value

        now = jnp.where(
            last,
            jnp.where(core == 0, chosen(orders[1][0]), chosen(orders[1][1])),
            jnp.where(core == 0, chosen(orders[0][0]), chosen(orders[0][1])),
        )
        kind = lax.div(now, 4)
        m = lax.rem(lax.div(now, 2), 2)
        chain = lax.rem(now, 2)
        pl.when(kind == FR)(lambda: forward_rows(m))
        pl.when(kind == FC)(lambda: forward_columns(m, chain))
        pl.when(kind == TR)(lambda: turn_rows(m))
        pl.when(kind == BC)(lambda: backward_columns(m, chain))
        pl.when((kind == BR) & jnp.logical_not(first))(lambda: backward_rows(m))
        pl.when(kind == TN)(lambda: turn_normed(m))
        return carry

    lax.fori_loop(0, 16, run, 0)

    own_gains = jnp.where(core == 0, gains[:, :half], gains[:, half:])
    gain_row[...] = jnp.sum(gain_sum[...], axis=0, keepdims=True) / own_gains

    def gain_send(step, carry):
        other = far_device(step)
        remote(
            gain_row, gain_in.at[me], gain_sem.at[0], gain_sem.at[1], section, other
        ).start()
        return carry

    lax.fori_loop(0, groups - 1, gain_send, 0)
    pltpu.make_async_copy(gain_row, gain_in.at[me], gain_sem.at[1]).start()

    arrived_copy = pltpu.make_async_copy(arrived, arrived_out, gain_sem.at[2])
    arrived_copy.start()
    weight_share.wait_send()
    for m in range(micro):
        for p in range(parts):
            await_bytes(back_in.at[m, p, 0 : groups - 1], gather_send.at[m])
        for chain in range(2):

            @pl.when(last & (core == chain))
            def _(m=m, chain=chain):
                await_bytes(pout.at[m, chain, 0 : chips - 1], part_send.at[m, chain])

            @pl.when(jnp.logical_not(last & (core == chain)))
            def _(m=m, chain=chain):
                await_bytes(pout.at[m, chain], part_send.at[m, chain])

            @pl.when(jnp.logical_not(first) & (core == chain))
            def _(m=m, chain=chain):
                await_bytes(back_out.at[m, chain, :, 0 : chips - 1], back_send.at[m, chain])

            @pl.when(jnp.logical_not(first) & (core != chain))
            def _(m=m, chain=chain):
                await_bytes(back_out.at[m, chain], back_send.at[m, chain])

            slope_copy(m, chain).wait()

        keep_share(m).wait()
        keep_own(m).wait()

        @pl.when(last)
        def _(m=m):
            await_bytes(pin.at[1, m, 0 : groups - 1], slope_send.at[1, m])

        @pl.when(jnp.logical_not(first))
        def _(m=m):
            await_bytes(pin.at[0, m], slope_send.at[0, m])

        @pl.when(section > 1)
        def _(m=m):
            await_bytes(up_out.at[m], side_send.at[1, m])

        @pl.when(jnp.logical_not(last))
        def _(m=m):
            await_bytes(arrived.at[m], side_send.at[0, m])

    await_bytes(gain_in, gain_sem.at[1])
    for side in range(2):
        total = gain_in[side]
        for q in range(1, chips):
            total = total + gain_in[2 * q + side]
        gain_full[:, side * half : (side + 1) * half] = total
    await_bytes(gain_in.at[0 : groups - 1], gain_sem.at[0])
    gain_copy = pltpu.make_async_copy(gain_full, gain_out, gain_sem.at[3])
    gain_copy.start()
    arrived_copy.wait()
    gain_copy.wait()


def on_device(sections, groups, acts_in, weights, gains, stored, sample_ids, cotangent):
    micro, seg_rows, width = acts_in.shape
    own_cols = weights.shape[2]
    half = width // 2
    chip_cols = 2 * own_cols
    chips = groups // 2
    rows = chips * seg_rows
    parts = 3
    span = half // parts
    anywhere = pl.BlockSpec(memory_space=pl.ANY)
    smem = pl.BlockSpec(memory_space=pltpu.SMEM)
    dma = pltpu.SemaphoreType.DMA
    arrived, normed, slope, gain = pl.pallas_call(
        functools.partial(relay, sections, groups),
        out_shape=(
            jax.ShapeDtypeStruct((micro, seg_rows, width), BF16),
            jax.ShapeDtypeStruct((width, micro * 2 * rows), BF16),
            jax.ShapeDtypeStruct((micro * 2 * rows, own_cols), BF16),
            jax.ShapeDtypeStruct((1, width), F32),
        ),
        in_specs=[smem] + [anywhere] * 5,
        out_specs=(anywhere,) * 4,
        scratch_shapes=[
            pltpu.VMEM((micro, seg_rows, width), BF16),
            pltpu.VMEM((1, width), F32),
            pltpu.VMEM(stored.shape, BF16),
            pltpu.VMEM((micro, seg_rows, width), BF16),
            pltpu.VMEM((half, chip_cols), BF16),
            pltpu.VMEM((micro, parts, 2, seg_rows, span), BF16),
            pltpu.VMEM((micro, 2, parts, chips, seg_rows, span), BF16),
            pltpu.VMEM((micro, 2, rows, half), BF16),
            pltpu.VMEM((micro, 2, chips, seg_rows, chip_cols), BF16),
            pltpu.VMEM((2, micro, groups, seg_rows, chip_cols), BF16),
            pltpu.VMEM((micro, seg_rows, width), F32),
            pltpu.VMEM((seg_rows, width), F32),
            pltpu.VMEM((micro, seg_rows, width), BF16),
            pltpu.VMEM((micro, seg_rows, width), BF16),
            pltpu.VMEM((2, micro, chips, seg_rows, chip_cols), BF16),
            pltpu.VMEM((micro, 2, chips, seg_rows, chip_cols), BF16),
            pltpu.VMEM((micro, 2, rows, chip_cols), BF16),
            pltpu.VMEM((micro, 2, parts, chips, seg_rows, span), BF16),
            pltpu.VMEM((micro, parts, groups, seg_rows, span), BF16),
            pltpu.VMEM((micro, seg_rows, width), BF16),
            pltpu.VMEM((micro, seg_rows, width), BF16),
            pltpu.VMEM((micro, seg_rows, 128), F32),
            pltpu.VMEM((micro, half, 2 * rows), BF16),
            pltpu.VMEM((rows, chip_cols), F32),
            pltpu.VMEM((seg_rows, half), F32),
            pltpu.VMEM((1, half), F32),
            pltpu.VMEM((groups, 1, half), F32),
            pltpu.VMEM((1, width), F32),
            dma((4,)),
            dma((3,)),
            dma((micro,)),
            dma((micro, 2, parts)),
            dma((micro, 2)),
            dma((2, micro)),
            dma((2, micro)),
            dma((micro, 2)),
            dma((micro, 2)),
            dma((micro,)),
            dma((2, micro)),
            dma((2, micro)),
            dma((micro,)),
            dma((micro,)),
            dma((2, micro, 2)),
            dma((4,)),
        ],
        compiler_params=pltpu.CompilerParams(
            collective_id=0, has_side_effects=True, vmem_limit_bytes=60 * 1024 * 1024
        ),
    )(sample_ids, acts_in, weights, gains, stored, cotangent)

    block_k = 512
    blocks = width // block_k
    slot_count = stored.shape[1]

    def finish(
        ids_ref, normed_ref, slope_ref, stored_ref, arrived_ref, gain_ref,
        kept_ref, grad_ref, total_ref,
        normed_buf, slope_buf, kept_buf, arrived_buf, grad_buf, in_sem, out_sem, side_sem,
    ):
        side = [
            pltpu.make_async_copy(slope_ref, slope_buf, side_sem.at[0]),
            pltpu.make_async_copy(stored_ref, kept_buf, side_sem.at[1]),
            pltpu.make_async_copy(arrived_ref, arrived_buf, side_sem.at[2]),
            pltpu.make_async_copy(gain_ref, total_ref, side_sem.at[3]),
        ]
        places = [pl.ds(b * block_k, block_k) for b in range(blocks)]
        takes = [
            pltpu.make_async_copy(normed_ref.at[place], normed_buf.at[place], in_sem.at[b])
            for b, place in enumerate(places)
        ]
        gives = [
            pltpu.make_async_copy(grad_buf.at[place], grad_ref.at[0, place], out_sem.at[b])
            for b, place in enumerate(places)
        ]
        side[0].start()
        for take in takes:
            take.start()
        for copy in side[1:]:
            copy.start()
        side[0].wait()
        for place, take, give in zip(places, takes, gives):
            take.wait()
            grad_buf[place] = jnp.dot(
                normed_buf[place], slope_buf[...], preferred_element_type=F32
            )
            give.start()
        side[1].wait()
        side[2].wait()
        for m in range(micro):
            slot = ids_ref[m, 0] - lax.axis_index("dp") * slot_count
            kept_buf[0, jnp.clip(slot, 0, slot_count - 1)] = arrived_buf[m]
        kept_copy = pltpu.make_async_copy(kept_buf, kept_ref, side_sem.at[4])
        kept_copy.start()
        side[3].wait()
        kept_copy.wait()
        for give in gives:
            give.wait()

    kept, grad, gain = pl.pallas_call(
        finish,
        out_shape=(
            jax.ShapeDtypeStruct(stored.shape, BF16),
            jax.ShapeDtypeStruct((1, width, own_cols), F32),
            jax.ShapeDtypeStruct((1, width), F32),
        ),
        in_specs=[smem] + [anywhere] * 5,
        out_specs=(anywhere,) * 3,
        scratch_shapes=[
            pltpu.VMEM(normed.shape, BF16),
            pltpu.VMEM(slope.shape, BF16),
            pltpu.VMEM(stored.shape, BF16),
            pltpu.VMEM(arrived.shape, BF16),
            pltpu.VMEM((width, own_cols), F32),
            dma((blocks,)),
            dma((blocks,)),
            dma((5,)),
        ],
        compiler_params=pltpu.CompilerParams(vmem_limit_bytes=60 * 1024 * 1024),
    )(sample_ids, normed, slope, stored, arrived, gain)
    return (kept, grad, gain)


def solution(mesh):
    placed = (
        P(None, "dp", None),
        P("section", None, "dp"),
        P("section", None),
        P("section", "dp", None, None),
        P(None, "dp"),
        P(None, "dp", None),
    )
    return jax.shard_map(
        functools.partial(on_device, mesh.shape["section"], mesh.shape["dp"]),
        mesh=mesh,
        in_specs=placed,
        out_specs=(P("section", "dp", None, None), P("section", None, "dp"), P("section", None)),
        check_vma=False,
    )
```

```python
import functools

import jax
import jax.numpy as jnp
from jax import lax
from jax.experimental import pallas as pl
from jax.experimental.pallas import tpu as pltpu
from jax.sharding import PartitionSpec as P

MESH = pl.DeviceIdType.MESH
F32 = jnp.float32
BF16 = jnp.bfloat16

clip_limit = 1.0
epsilon = 1e-05
gelu_coeff = 0.7978845608028654


def gelu_value(values):
    inner = gelu_coeff * (values + 0.044715 * values * values * values)
    return 0.5 * values * (1.0 + jnp.tanh(inner))


def gelu_slope(values):
    tangent = jnp.tanh(gelu_coeff * (values + 0.044715 * values * values * values))
    return 0.5 * (1.0 + tangent) + 0.5 * values * (1.0 - tangent * tangent) * gelu_coeff * (
        1.0 + 0.134145 * values * values
    )


part_count = 2
step_b = 256
stagger_us, gather_us, turn_us, slope_us, back_us = 3.5, 5.5, 5.5, 4.6, 6.4


def make_order(micro, turning, side):
    FR, FC, TR, BC, BR, TN = range(6)
    events = []
    for k in range(4 * micro):
        start = stagger_us * k
        back = start + gather_us + turn_us + slope_us if turning else start + 1000.0
        events.append((start + gather_us, FC * 8 + k))
        events.append((back, BC * 8 + k))
        if k % 2 == side:
            events.append((start, FR * 8 + k))
            events.append((back + back_us, BR * 8 + k))
            if turning:
                events.append((start + gather_us + turn_us, TR * 8 + k))
    for m in range(micro):
        events.append((2000.0 if turning else 500.0, TN * 8 + 4 * m))
    return [entry for _, entry in sorted(events)]


def relay(
    sections,
    groups,
    ids,
    acts_hbm,
    weights,
    gains_hbm,
    stored_hbm,
    cotangent_hbm,
    arrived_out,
    normed_out,
    slope_out,
    gain_out,
    acts,
    gains,
    stored,
    cotangent,
    acts_p,
    before_p,
    cotangent_p,
    gains_p,
    wbuf,
    nbuf,
    gbuf,
    xbuf,
    products,
    pout,
    pin,
    hidden,
    incoming,
    arrived,
    arrived_whole,
    arr_in,
    slopes,
    slope_in,
    ybuf,
    own_slope,
    back_out,
    back_in,
    up_in,
    up_out,
    scales,
    xturned,
    gain_sum,
    gain_row,
    gain_in,
    gain_full,
    load_sem,
    w_sem,
    gather_send,
    gather_recv,
    part_send,
    part_recv,
    slope_send,
    slope_recv,
    back_send,
    back_recv,
    side_send,
    side_recv,
    keep_send,
    keep_recv,
    keep_sem,
    copy_sem,
    gain_sem,
    stagger,
):
    micro, seg_rows, width = acts.shape
    half = width // 2
    fold = half // 2
    own_cols = weights.shape[2]
    chip_cols = 2 * own_cols
    chips = groups // 2
    quarter = chips // 2
    rows = chips * seg_rows
    slot_count = stored.shape[1]
    sets = 2 * micro
    parts = gbuf.shape[2]
    span = fold // parts
    section = lax.axis_index("section")
    me = lax.axis_index("dp")
    core = lax.rem(me, 2)
    chip = lax.div(me, 2)
    sibling = me + 1 - 2 * core
    first = section == 0
    last = section == sections - 1
    after = lax.rem(section + 1, sections)
    before = lax.rem(section + sections - 1, sections)
    z_count = groups // 4
    z_pos = lax.div(me, 4)
    x_pos = lax.rem(chip, 2)

    loads = [
        pltpu.make_async_copy(source, target, load_sem.at[i])
        for i, (source, target) in enumerate(
            (
                (acts_hbm, acts),
                (stored_hbm, stored),
                (gains_hbm, gains),
                (cotangent_hbm, cotangent),
            )
        )
    ]
    for load in loads:
        load.start()
    own_place = pl.ds(pl.multiple_of(core * own_cols, 128), own_cols)

    def weight_pieces(side):
        for q in range(quarter):
            for h in range(2):
                yield (
                    weights.at[
                        0, pl.ds(side * half + q * chip_cols + h * own_cols, own_cols), :
                    ],
                    wbuf.at[h, q * own_cols : (q + 1) * own_cols, own_place],
                )

    for source, target in weight_pieces(core):
        pltpu.make_async_copy(source, target, w_sem.at[2]).start()

    barrier = pltpu.get_barrier_semaphore()

    def greet(step, carry):
        other = lax.rem(me + step, groups)
        for there in (after, before):
            pl.semaphore_signal(
                barrier, inc=1, device_id={"section": there, "dp": other}, device_id_type=MESH
            )

        @pl.when(step > 0)
        def _():
            pl.semaphore_signal(
                barrier, inc=1, device_id={"section": section, "dp": other}, device_id_type=MESH
            )

        return carry

    lax.fori_loop(0, groups, greet, 0)

    def part(q):
        return slice(q * own_cols, (q + 1) * own_cols)

    def low_rows(shape):
        return lax.broadcasted_iota(jnp.int32, shape, len(shape) - 2) < 4

    def turned(value):
        return pltpu.roll(value, 4, axis=value.ndim - 2)

    def columns(q, h):
        start = q * chip_cols + h * own_cols
        return slice(start, start + own_cols)

    def pack(value, target, index):
        for q in range(chips):
            left, right = value[:, columns(q, 0)], value[:, columns(q, 1)]
            low = low_rows(left.shape)
            target[index, :, part(q)] = jnp.where(low, left, turned(right)).astype(target.dtype)
            target[index + 1, :, part(q)] = jnp.where(low, turned(left), right).astype(
                target.dtype
            )

    def unpack(one, two):
        low = low_rows(one.shape)
        return jnp.where(low, one, turned(two)), jnp.where(low, turned(one), two)

    for load in loads:
        load.wait()
    for q in range(chips):
        left = jnp.broadcast_to(gains[:, columns(q, 0)], (seg_rows, own_cols))
        right = jnp.broadcast_to(gains[:, columns(q, 1)], (seg_rows, own_cols))
        gains_p[:, part(q)] = jnp.where(low_rows(left.shape), left, right)
    for m in range(micro):
        slot = jnp.clip(ids[m, 0] - me * slot_count, 0, slot_count - 1)
        pack(acts[m].astype(F32), acts_p, 2 * m)
        pack(stored[0, slot].astype(F32), before_p, 2 * m)
        pack(cotangent[m].astype(F32), cotangent_p, 2 * m)
    gain_sum[...] = jnp.zeros_like(gain_sum)
    pl.semaphore_wait(barrier, 3 * groups - 1)

    def remote(source, target, send, recv, there, other):
        return pltpu.make_async_remote_copy(
            src_ref=source,
            dst_ref=target,
            send_sem=send,
            recv_sem=recv,
            device_id={"section": there, "dp": other},
            device_id_type=MESH,
        )

    for source, target in weight_pieces(1 - core):
        remote(source, target, w_sem.at[0], w_sem.at[1], section, sibling).start()

    def far_z(i):
        away = jnp.where(i == 3, 0, jnp.where(i == 0, 2, 2 * i - 1))
        return lax.rem(z_pos + away, z_count)

    def far_device(i):
        x = lax.rem(x_pos + 1 - lax.rem(lax.div(i, 2), 2), 2)
        return far_z(lax.div(i, 4)) * 4 + x * 2 + lax.rem(core + 1 - lax.rem(i, 2), 2)

    def far_chip(i):
        return far_z(lax.div(i, 2)) * 2 + lax.rem(x_pos + 1 - lax.rem(i, 2), 2)

    def await_bytes(ref, sem):
        pltpu.make_async_copy(ref, ref, sem).wait()

    def row_mean(value):
        total = jnp.broadcast_to(jnp.sum(value, axis=-1, keepdims=True), (seg_rows, 128))
        return ((total + turned(total)) / width)[:, :1]

    def turned_place(m):
        wide = 2 * rows
        return (
            pl.ds(pl.multiple_of(core * half, half), half),
            pl.ds(pl.multiple_of(m * wide, wide), wide),
        )

    def keep_share(m):
        return remote(
            xturned.at[m],
            normed_out.at[turned_place(m)],
            keep_send.at[m],
            keep_recv.at[m],
            section,
            sibling,
        )

    def keep_own(m):
        return pltpu.make_async_copy(xturned.at[m], normed_out.at[turned_place(m)], keep_sem.at[m])

    def turn_normed(m):
        for q in range(quarter):
            p, start = (q * own_cols) // span, (q * own_cols) % span
            sides = [[], []]
            for chain in range(2):
                one, two = (
                    gbuf[2 * m + u, chain, p, :, :, start : start + own_cols].astype(F32)
                    for u in range(2)
                )
                for h, whole in enumerate(unpack(one, two)):
                    sides[h].append(whole.reshape(rows, own_cols))
            for h in range(2):
                piece = jnp.transpose(jnp.concatenate(sides[h], axis=0))
                xturned[m, columns(q, h), :] = piece.astype(BF16)
        keep_share(m).start()
        keep_own(m).start()

    def slope_copy(m, chain):
        return pltpu.make_async_copy(
            own_slope.at[m, chain],
            slope_out.at[pl.ds(pl.multiple_of((m * 2 + chain) * rows, rows), rows), :],
            copy_sem.at[m, chain],
        )

    def send_slopes(kind, e, there, remote_own):
        def send(step, carry):
            other = far_device(step)
            remote(
                slopes.at[kind, e, lax.div(other, 2)],
                slope_in.at[e, core, chip],
                slope_send.at[kind, e],
                slope_recv.at[e, core],
                there,
                other,
            ).start()
            return carry

        if remote_own:
            lax.fori_loop(0, groups, send, 0)
        else:
            lax.fori_loop(0, groups - 1, send, 0)
            pltpu.make_async_copy(
                slopes.at[kind, e, chip], slope_in.at[e, core, chip], slope_recv.at[e, core]
            ).start()

    def summed_parts(kind, e, q):
        return pin[kind, e, 2 * q].astype(F32) + pin[kind, e, 2 * q + 1].astype(F32)

    def forward_rows(e):
        @pl.when(first & (e == 0) & (core == 1))
        def _():
            pl.semaphore_wait(stagger, 1)

        @pl.when(first)
        def _():
            incoming[...] = acts_p[e]

        @pl.when(jnp.logical_not(first))
        def _():
            await_bytes(arr_in.at[e], side_recv.at[0, e])
            await_bytes(pin.at[0, e], part_recv.at[0, e])
            for q in range(chips):
                value = summed_parts(0, e, q)
                hidden[e, :, part(q)] = value
                total = arr_in[e, :, part(q)].astype(F32) + gelu_value(value)
                incoming[:, part(q)] = total.astype(BF16).astype(F32)

        previous = before_p[e]
        moved = jnp.clip(incoming[...] - previous, -clip_limit, clip_limit)
        arrived_now = (previous + moved).astype(BF16)
        arrived[e] = arrived_now
        arrived_f = arrived_now.astype(F32)
        scale = lax.rsqrt(row_mean(arrived_f * arrived_f) + epsilon)
        scales[e] = jnp.broadcast_to(scale, (seg_rows, 128))
        normed = (arrived_f * scale * gains_p[...]).astype(BF16)
        for side in range(2):
            for p in range(parts):
                start = side * fold + p * span
                nbuf[e, p, side] = normed[:, start : start + span]
        for p in range(parts):

            def send(step, carry, p=p):
                other = far_device(step)
                remote(
                    nbuf.at[e, p, lax.rem(other, 2)],
                    gbuf.at[e, core, p, chip],
                    gather_send.at[e],
                    gather_recv.at[e, core, p],
                    section,
                    other,
                ).start()
                return carry

            lax.fori_loop(0, groups - 1, send, 0)
            pltpu.make_async_copy(
                nbuf.at[e, p, core], gbuf.at[e, core, p, chip], gather_recv.at[e, core, p]
            ).start()

        @pl.when(jnp.logical_not(last))
        def _():
            remote(
                arrived.at[e], arr_in.at[e], side_send.at[0, e], side_recv.at[0, e], after, me
            ).start()

        @pl.when(jnp.logical_not(first))
        def _():
            for q in range(chips):
                hidden[e, :, part(q)] = gelu_slope(hidden[e, :, part(q)])

    def forward_columns(e, chain):
        @pl.when((e == 0) & (chain == 0))
        def _():
            await_bytes(wbuf.at[:, :, own_place], w_sem.at[2])
            await_bytes(wbuf.at[:, :, own_place], w_sem.at[1])

        for p in range(parts):
            await_bytes(gbuf.at[e, chain, p], gather_recv.at[e, chain, p])
            if p == 0:

                @pl.when(first & (e == 0) & (chain == 0) & (core == 0))
                def _():
                    pl.semaphore_signal(
                        stagger, inc=1, device_id={"dp": sibling}, device_id_type=MESH
                    )

            base = p * span
            piece = gbuf[e, chain, p].astype(F32).reshape(rows, span)
            xbuf[:, base : base + span] = piece.astype(BF16)
            for h in range(2):
                for c in range(0, chip_cols, 256):
                    product = jnp.dot(
                        xbuf[:, base : base + span],
                        wbuf[h, base : base + span, c : c + 256],
                        preferred_element_type=F32,
                    )
                    if p > 0:
                        product = product + products[h, :, c : c + 256]
                    products[h, :, c : c + 256] = product
        shape = (chips, seg_rows, own_cols)
        left = products[0, :, :own_cols].reshape(shape) + turned(
            products[1, :, :own_cols].reshape(shape)
        )
        right = (
            turned(products[0, :, own_cols:].reshape(shape))
            + products[1, :, own_cols:].reshape(shape)
        )
        pout[e, chain] = jnp.where(low_rows(shape), left, right).astype(BF16)

        def send(step, carry):
            q = far_chip(step)
            other = 2 * q + chain

            @pl.when(jnp.logical_not(last))
            def _():
                remote(
                    pout.at[e, chain, q],
                    pin.at[0, e, me],
                    part_send.at[e, chain],
                    part_recv.at[0, e],
                    after,
                    other,
                ).start()

            @pl.when(last & (other != me))
            def _():
                remote(
                    pout.at[e, chain, q],
                    pin.at[1, e, me],
                    part_send.at[e, chain],
                    part_recv.at[1, e],
                    section,
                    other,
                ).start()

            return carry

        lax.fori_loop(0, chips, send, 0)

        @pl.when(last & (core == chain))
        def _():
            pltpu.make_async_copy(
                pout.at[e, chain, chip], pin.at[1, e, me], part_recv.at[1, e]
            ).start()

    def turn_rows(e):
        await_bytes(pin.at[1, e], part_recv.at[1, e])
        for q in range(chips):
            slope = cotangent_p[e, :, part(q)].astype(F32) * gelu_slope(summed_parts(1, e, q))
            slopes[1, e, q] = slope.astype(BF16)
        send_slopes(1, e, section, False)

    def backward_columns(e, chain):
        await_bytes(slope_in.at[e, chain], slope_recv.at[e, chain])
        ybuf[...] = slope_in[e, chain].astype(F32).reshape(rows, own_cols).astype(BF16)
        for p in range(parts):
            for k in range(0, span, step_b):
                start = p * span + k
                shape = (chips, seg_rows, step_b)
                terms = [
                    [
                        lax.dot_general(
                            ybuf[...],
                            wbuf[h, start : start + step_b, s * own_cols : (s + 1) * own_cols],
                            (((1,), (1,)), ((), ())),
                            preferred_element_type=F32,
                        ).reshape(shape)
                        for s in range(2)
                    ]
                    for h in range(2)
                ]
                left = terms[0][0] + turned(terms[0][1])
                right = turned(terms[1][0]) + terms[1][1]
                back_out[e, chain, p, :, :, k : k + step_b] = jnp.where(
                    low_rows(shape), left, right
                ).astype(BF16)

            def send(step, carry, p=p):
                q = far_chip(step)
                other = 2 * q + chain

                @pl.when(other != me)
                def _():
                    remote(
                        back_out.at[e, chain, p, q],
                        back_in.at[e, p, me],
                        back_send.at[e, chain],
                        back_recv.at[e],
                        section,
                        other,
                    ).start()

                return carry

            @pl.when(jnp.logical_not(first))
            def _(p=p, send=send):
                lax.fori_loop(0, chips, send, 0)

            @pl.when(jnp.logical_not(first) & (core == chain))
            def _(p=p):
                pltpu.make_async_copy(
                    back_out.at[e, chain, p, chip], back_in.at[e, p, me], back_recv.at[e]
                ).start()

        for p in range(parts):
            term = back_out[e, chain, p].astype(F32) * gbuf[e, chain, p].astype(F32)
            gain_sum[:, p * span : (p + 1) * span] += jnp.sum(term, axis=0)

        @pl.when(lax.rem(e, 2) == 1)
        def _():
            m = lax.div(e, 2)
            left, right = unpack(
                slope_in[e - 1, chain].astype(F32), slope_in[e, chain].astype(F32)
            )
            mine = jnp.where(core == 0, left, right).reshape(rows, own_cols)
            own_slope[m, chain] = mine.astype(BF16)
            slope_copy(m, chain).start()

    def backward_rows(e):
        @pl.when(last)
        def _():
            up_in[e] = cotangent_p[e]

        @pl.when(jnp.logical_not(last))
        def _():
            await_bytes(up_in.at[e], side_recv.at[1, e])

        await_bytes(back_in.at[e], back_recv.at[e])
        pieces = []
        for side in range(2):
            for p in range(parts):
                total = back_in[e, p, side].astype(F32)
                for q in range(1, chips):
                    total = total + back_in[e, p, 2 * q + side].astype(F32)
                pieces.append(total)
        back = jnp.concatenate(pieces, axis=1)
        arrived_f = arrived[e].astype(F32)
        scale = scales[e][:, :1]
        weighted = back * gains_p[...]
        mean_term = row_mean(weighted * arrived_f)
        total = up_in[e].astype(F32) + scale * (weighted - arrived_f * scale * scale * mean_term)
        up_out[e] = total.astype(BF16)
        for q in range(chips):
            slope = up_out[e, :, part(q)].astype(F32) * hidden[e, :, part(q)]
            slopes[0, e, q] = slope.astype(BF16)
        send_slopes(0, e, before, True)

        @pl.when(section > 1)
        def _():
            remote(
                up_out.at[e], up_in.at[e], side_send.at[1, e], side_recv.at[1, e], before, me
            ).start()

    FR, FC, TR, BC, BR, TN, NO = range(7)
    orders = [[make_order(micro, where, side) for side in range(2)] for where in range(2)]
    length = max(len(order) for pair in orders for order in pair)
    for pair in orders:
        for order in pair:
            order += [NO * 8] * (length - len(order))

    def run(t, carry):
        now = NO * 8
        for i in range(length):
            here = jnp.where(
                last,
                jnp.where(core == 0, orders[1][0][i], orders[1][1][i]),
                jnp.where(core == 0, orders[0][0][i], orders[0][1][i]),
            )
            now = jnp.where(t == i, here, now)
        kind = lax.div(now, 8)
        e = lax.rem(lax.div(now, 2), sets)
        chain = lax.rem(now, 2)
        pl.when(kind == FR)(lambda: forward_rows(e))
        pl.when(kind == FC)(lambda: forward_columns(e, chain))
        pl.when(kind == TR)(lambda: turn_rows(e))
        pl.when(kind == BC)(lambda: backward_columns(e, chain))
        pl.when((kind == BR) & jnp.logical_not(first))(lambda: backward_rows(e))
        pl.when(kind == TN)(lambda: turn_normed(lax.div(e, 2)))
        return carry

    lax.fori_loop(0, length, run, 0)

    low = low_rows(gain_sum.shape)
    sums = gain_sum[...]
    left = jnp.sum(jnp.where(low, sums, 0.0), axis=0, keepdims=True)
    right = jnp.sum(jnp.where(low, 0.0, sums), axis=0, keepdims=True)
    own_gains = jnp.where(core == 0, gains[:, :half], gains[:, half:])
    for q in range(quarter):
        for h, value in enumerate((left, right)):
            gain_row[:, columns(q, h)] = value[:, part(q)] / own_gains[:, columns(q, h)]

    def gain_send(step, carry):
        other = far_device(step)
        remote(
            gain_row, gain_in.at[me], gain_sem.at[0], gain_sem.at[1], section, other
        ).start()
        return carry

    lax.fori_loop(0, groups - 1, gain_send, 0)
    pltpu.make_async_copy(gain_row, gain_in.at[me], gain_sem.at[1]).start()

    for m in range(micro):
        for q in range(chips):
            wholes = unpack(
                arrived[2 * m, :, part(q)].astype(F32), arrived[2 * m + 1, :, part(q)].astype(F32)
            )
            for h, whole in enumerate(wholes):
                arrived_whole[m, :, columns(q, h)] = whole.astype(BF16)
    arrived_copy = pltpu.make_async_copy(arrived_whole, arrived_out, gain_sem.at[2])
    arrived_copy.start()
    await_bytes(wbuf.at[:, :, own_place], w_sem.at[0])
    for e in range(sets):
        for p in range(parts):
            await_bytes(back_in.at[e, p, 0 : groups - 1], gather_send.at[e])
        for chain in range(2):

            @pl.when(last & (core == chain))
            def _(e=e, chain=chain):
                await_bytes(pout.at[e, chain, 0 : chips - 1], part_send.at[e, chain])

            @pl.when(jnp.logical_not(last & (core == chain)))
            def _(e=e, chain=chain):
                await_bytes(pout.at[e, chain], part_send.at[e, chain])

            @pl.when(jnp.logical_not(first) & (core == chain))
            def _(e=e, chain=chain):
                await_bytes(back_out.at[e, chain, :, 0 : chips - 1], back_send.at[e, chain])

            @pl.when(jnp.logical_not(first) & (core != chain))
            def _(e=e, chain=chain):
                await_bytes(back_out.at[e, chain], back_send.at[e, chain])

        @pl.when(last)
        def _(e=e):
            await_bytes(pin.at[1, e, 0 : groups - 1], slope_send.at[1, e])

        @pl.when(jnp.logical_not(first))
        def _(e=e):
            await_bytes(pin.at[0, e], slope_send.at[0, e])

        @pl.when(section > 1)
        def _(e=e):
            await_bytes(up_out.at[e], side_send.at[1, e])

        @pl.when(jnp.logical_not(last))
        def _(e=e):
            await_bytes(arrived.at[e], side_send.at[0, e])

    for m in range(micro):
        for chain in range(2):
            slope_copy(m, chain).wait()
        keep_share(m).wait()
        keep_own(m).wait()

    await_bytes(gain_in, gain_sem.at[1])
    for side in range(2):
        total = gain_in[side]
        for q in range(1, chips):
            total = total + gain_in[2 * q + side]
        gain_full[:, side * half : (side + 1) * half] = total
    await_bytes(gain_in.at[0 : groups - 1], gain_sem.at[0])
    gain_copy = pltpu.make_async_copy(gain_full, gain_out, gain_sem.at[3])
    gain_copy.start()
    arrived_copy.wait()
    gain_copy.wait()


def on_device(sections, groups, acts_in, weights, gains, stored, sample_ids, cotangent):
    micro, seg_rows, width = acts_in.shape
    own_cols = weights.shape[2]
    half = width // 2
    fold = half // 2
    chip_cols = 2 * own_cols
    chips = groups // 2
    rows = chips * seg_rows
    sets = 2 * micro
    parts = part_count
    span = fold // parts
    anywhere = pl.BlockSpec(memory_space=pl.ANY)
    smem = pl.BlockSpec(memory_space=pltpu.SMEM)
    dma = pltpu.SemaphoreType.DMA
    arrived, normed, slope, gain = pl.pallas_call(
        functools.partial(relay, sections, groups),
        out_shape=(
            jax.ShapeDtypeStruct((micro, seg_rows, width), BF16),
            jax.ShapeDtypeStruct((width, micro * 2 * rows), BF16),
            jax.ShapeDtypeStruct((micro * 2 * rows, own_cols), BF16),
            jax.ShapeDtypeStruct((1, width), F32),
        ),
        in_specs=[smem] + [anywhere] * 5,
        out_specs=(anywhere,) * 4,
        scratch_shapes=[
            pltpu.VMEM((micro, seg_rows, width), BF16),
            pltpu.VMEM((1, width), F32),
            pltpu.VMEM(stored.shape, BF16),
            pltpu.VMEM((micro, seg_rows, width), BF16),
            pltpu.VMEM((sets, seg_rows, half), F32),
            pltpu.VMEM((sets, seg_rows, half), F32),
            pltpu.VMEM((sets, seg_rows, half), BF16),
            pltpu.VMEM((seg_rows, half), F32),
            pltpu.VMEM((2, fold, chip_cols), BF16),
            pltpu.VMEM((sets, parts, 2, seg_rows, span), BF16),
            pltpu.VMEM((sets, 2, parts, chips, seg_rows, span), BF16),
            pltpu.VMEM((rows, fold), BF16),
            pltpu.VMEM((2, rows, chip_cols), F32),
            pltpu.VMEM((sets, 2, chips, seg_rows, own_cols), BF16),
            pltpu.VMEM((2, sets, groups, seg_rows, own_cols), BF16),
            pltpu.VMEM((sets, seg_rows, half), F32),
            pltpu.VMEM((seg_rows, half), F32),
            pltpu.VMEM((sets, seg_rows, half), BF16),
            pltpu.VMEM((micro, seg_rows, width), BF16),
            pltpu.VMEM((sets, seg_rows, half), BF16),
            pltpu.VMEM((2, sets, chips, seg_rows, own_cols), BF16),
            pltpu.VMEM((sets, 2, chips, seg_rows, own_cols), BF16),
            pltpu.VMEM((rows, own_cols), BF16),
            pltpu.VMEM((micro, 2, rows, own_cols), BF16),
            pltpu.VMEM((sets, 2, parts, chips, seg_rows, span), BF16),
            pltpu.VMEM((sets, parts, groups, seg_rows, span), BF16),
            pltpu.VMEM((sets, seg_rows, half), BF16),
            pltpu.VMEM((sets, seg_rows, half), BF16),
            pltpu.VMEM((sets, seg_rows, 128), F32),
            pltpu.VMEM((micro, half, 2 * rows), BF16),
            pltpu.VMEM((seg_rows, fold), F32),
            pltpu.VMEM((1, half), F32),
            pltpu.VMEM((groups, 1, half), F32),
            pltpu.VMEM((1, width), F32),
            dma((4,)),
            dma((3,)),
            dma((sets,)),
            dma((sets, 2, parts)),
            dma((sets, 2)),
            dma((2, sets)),
            dma((2, sets)),
            dma((sets, 2)),
            dma((sets, 2)),
            dma((sets,)),
            dma((2, sets)),
            dma((2, sets)),
            dma((micro,)),
            dma((micro,)),
            dma((micro,)),
            dma((micro, 2)),
            dma((4,)),
            pltpu.SemaphoreType.REGULAR,
        ],
        compiler_params=pltpu.CompilerParams(
            collective_id=0, has_side_effects=True, vmem_limit_bytes=60 * 1024 * 1024
        ),
    )(sample_ids, acts_in, weights, gains, stored, cotangent)

    block_k = 512
    blocks = width // block_k
    slot_count = stored.shape[1]

    def finish(
        ids_ref, normed_ref, slope_ref, stored_ref, arrived_ref, gain_ref,
        kept_ref, grad_ref, total_ref,
        normed_buf, slope_buf, kept_buf, arrived_buf, grad_buf, in_sem, out_sem, side_sem,
    ):
        side = [
            pltpu.make_async_copy(slope_ref, slope_buf, side_sem.at[0]),
            pltpu.make_async_copy(stored_ref, kept_buf, side_sem.at[1]),
            pltpu.make_async_copy(arrived_ref, arrived_buf, side_sem.at[2]),
            pltpu.make_async_copy(gain_ref, total_ref, side_sem.at[3]),
        ]
        places = [pl.ds(b * block_k, block_k) for b in range(blocks)]
        takes = [
            pltpu.make_async_copy(normed_ref.at[place], normed_buf.at[place], in_sem.at[b])
            for b, place in enumerate(places)
        ]
        gives = [
            pltpu.make_async_copy(grad_buf.at[place], grad_ref.at[0, place], out_sem.at[b])
            for b, place in enumerate(places)
        ]
        side[0].start()
        for take in takes:
            take.start()
        for copy in side[1:]:
            copy.start()
        side[0].wait()
        for place, take, give in zip(places, takes, gives):
            take.wait()
            grad_buf[place] = jnp.dot(
                normed_buf[place], slope_buf[...], preferred_element_type=F32
            )
            give.start()
        side[1].wait()
        side[2].wait()
        for m in range(micro):
            slot = ids_ref[m, 0] - lax.axis_index("dp") * slot_count
            kept_buf[0, jnp.clip(slot, 0, slot_count - 1)] = arrived_buf[m]
        kept_copy = pltpu.make_async_copy(kept_buf, kept_ref, side_sem.at[4])
        kept_copy.start()
        side[3].wait()
        kept_copy.wait()
        for give in gives:
            give.wait()

    kept, grad, gain = pl.pallas_call(
        finish,
        out_shape=(
            jax.ShapeDtypeStruct(stored.shape, BF16),
            jax.ShapeDtypeStruct((1, width, own_cols), F32),
            jax.ShapeDtypeStruct((1, width), F32),
        ),
        in_specs=[smem] + [anywhere] * 5,
        out_specs=(anywhere,) * 3,
        scratch_shapes=[
            pltpu.VMEM(normed.shape, BF16),
            pltpu.VMEM(slope.shape, BF16),
            pltpu.VMEM(stored.shape, BF16),
            pltpu.VMEM(arrived.shape, BF16),
            pltpu.VMEM((width, own_cols), F32),
            dma((blocks,)),
            dma((blocks,)),
            dma((5,)),
        ],
        compiler_params=pltpu.CompilerParams(vmem_limit_bytes=60 * 1024 * 1024),
    )(sample_ids, normed, slope, stored, arrived, gain)
    return (kept, grad, gain)


def solution(mesh):
    placed = (
        P(None, "dp", None),
        P("section", None, "dp"),
        P("section", None),
        P("section", "dp", None, None),
        P(None, "dp"),
        P(None, "dp", None),
    )
    return jax.shard_map(
        functools.partial(on_device, mesh.shape["section"], mesh.shape["dp"]),
        mesh=mesh,
        in_specs=placed,
        out_specs=(P("section", "dp", None, None), P("section", None, "dp"), P("section", None)),
        check_vma=False,
    )
```

```python
import functools

import jax
import jax.numpy as jnp
from jax import lax
from jax.experimental import pallas as pl
from jax.experimental.pallas import tpu as pltpu
from jax.sharding import PartitionSpec as P

MESH = pl.DeviceIdType.MESH
F32 = jnp.float32
BF16 = jnp.bfloat16

clip_limit = 1.0
epsilon = 1e-05
gelu_coeff = 0.7978845608028654


def gelu_value(values):
    inner = gelu_coeff * (values + 0.044715 * values * values * values)
    return 0.5 * values * (1.0 + jnp.tanh(inner))


def gelu_slope(values):
    tangent = jnp.tanh(gelu_coeff * (values + 0.044715 * values * values * values))
    return 0.5 * (1.0 + tangent) + 0.5 * values * (1.0 - tangent * tangent) * gelu_coeff * (
        1.0 + 0.134145 * values * values
    )


gather_cuts = (0, 768, 1280, 1536)
back_cuts = (0, 512, 1024, 1536)
step_b = 256
plain_us = (3.5, 5.5, 2.8, 6.4, 0.0)
turning_us = (3.5, 5.5, 1.4, 6.4, 0.0)


def make_order(micro, turning, side):
    FR, FC, BC, BR, TN = range(5)
    stagger_us, gather_us, pair_us, back_us, late_us = turning_us if turning else plain_us
    events = []
    for k in range(4 * micro):
        start = stagger_us * k
        back = start + gather_us + pair_us if turning else start + 1000.0
        events.append((start + gather_us, FC * 8 + k))
        events.append((back, BC * 8 + k))
        if k % 2 == side:
            events.append((start + (late_us if k >= 4 else 0.0), FR * 8 + k))
            events.append((back + back_us, BR * 8 + k))
    for m in range(micro):
        events.append((2000.0 if turning else 500.0, TN * 8 + 4 * m))
    return [entry for _, entry in sorted(events)]


def relay(
    sections,
    groups,
    ids,
    acts_hbm,
    weights,
    gains_hbm,
    stored_hbm,
    cotangent_hbm,
    arrived_out,
    normed_out,
    slope_out,
    gain_out,
    acts,
    gains,
    stored,
    cotangent,
    acts_p,
    before_p,
    cotangent_p,
    gains_p,
    wbuf,
    nbuf,
    gbuf,
    xbuf,
    products,
    pout,
    pin,
    pair_in,
    hidden,
    incoming,
    arrived,
    arrived_whole,
    arr_in,
    slopes,
    slope_in,
    ybuf,
    own_slope,
    back_out,
    back_in,
    up_in,
    up_out,
    scales,
    xturned,
    gain_sum,
    gain_row,
    gain_in,
    gain_full,
    load_sem,
    w_sem,
    gather_send,
    gather_recv,
    part_send,
    part_recv,
    pair_recv,
    slope_send,
    slope_recv,
    back_send,
    back_recv,
    side_send,
    side_recv,
    keep_send,
    keep_recv,
    keep_sem,
    copy_sem,
    gain_sem,
    stagger,
):
    micro, seg_rows, width = acts.shape
    half = width // 2
    fold = half // 2
    own_cols = weights.shape[2]
    chip_cols = 2 * own_cols
    chips = groups // 2
    quarter = chips // 2
    rows = chips * seg_rows
    slot_count = stored.shape[1]
    sets = 2 * micro
    gather_parts = list(zip(gather_cuts[:-1], gather_cuts[1:]))
    back_parts = list(zip(back_cuts[:-1], back_cuts[1:]))
    section = lax.axis_index("section")
    me = lax.axis_index("dp")
    core = lax.rem(me, 2)
    chip = lax.div(me, 2)
    sibling = me + 1 - 2 * core
    first = section == 0
    last = section == sections - 1
    after = lax.rem(section + 1, sections)
    before = lax.rem(section + sections - 1, sections)
    z_count = groups // 4
    z_pos = lax.div(me, 4)
    x_pos = lax.rem(chip, 2)

    loads = [
        pltpu.make_async_copy(source, target, load_sem.at[i])
        for i, (source, target) in enumerate(
            (
                (acts_hbm, acts),
                (stored_hbm, stored),
                (gains_hbm, gains),
                (cotangent_hbm, cotangent),
            )
        )
    ]
    for load in loads:
        load.start()
    own_place = pl.ds(pl.multiple_of(core * own_cols, 128), own_cols)

    def weight_pieces(side):
        for q in range(quarter):
            for h in range(2):
                yield (
                    weights.at[
                        0, pl.ds(side * half + q * chip_cols + h * own_cols, own_cols), :
                    ],
                    wbuf.at[h, q * own_cols : (q + 1) * own_cols, own_place],
                )

    for source, target in weight_pieces(core):
        pltpu.make_async_copy(source, target, w_sem.at[2]).start()

    barrier = pltpu.get_barrier_semaphore()

    def greet(step, carry):
        other = lax.rem(me + step, groups)
        for there in (after, before):
            pl.semaphore_signal(
                barrier, inc=1, device_id={"section": there, "dp": other}, device_id_type=MESH
            )

        @pl.when(step > 0)
        def _():
            pl.semaphore_signal(
                barrier, inc=1, device_id={"section": section, "dp": other}, device_id_type=MESH
            )

        return carry

    lax.fori_loop(0, groups, greet, 0)

    def part(q):
        return slice(q * own_cols, (q + 1) * own_cols)

    def low_rows(shape):
        return lax.broadcasted_iota(jnp.int32, shape, len(shape) - 2) < 4

    def turned(value):
        return pltpu.roll(value, 4, axis=value.ndim - 2)

    def columns(q, h):
        start = q * chip_cols + h * own_cols
        return slice(start, start + own_cols)

    def pack(value, target, index):
        for q in range(chips):
            left, right = value[:, columns(q, 0)], value[:, columns(q, 1)]
            low = low_rows(left.shape)
            target[index, :, part(q)] = jnp.where(low, left, turned(right)).astype(target.dtype)
            target[index + 1, :, part(q)] = jnp.where(low, turned(left), right).astype(
                target.dtype
            )

    def unpack(one, two):
        low = low_rows(one.shape)
        return jnp.where(low, one, turned(two)), jnp.where(low, turned(one), two)

    for load in loads:
        load.wait()
    for q in range(chips):
        left = jnp.broadcast_to(gains[:, columns(q, 0)], (seg_rows, own_cols))
        right = jnp.broadcast_to(gains[:, columns(q, 1)], (seg_rows, own_cols))
        gains_p[:, part(q)] = jnp.where(low_rows(left.shape), left, right)
    for m in range(micro):
        slot = jnp.clip(ids[m] - me * slot_count, 0, slot_count - 1)
        pack(acts[m].astype(F32), acts_p, 2 * m)
        pack(stored[0, slot].astype(F32), before_p, 2 * m)
        pack(cotangent[m].astype(F32), cotangent_p, 2 * m)
    gain_sum[...] = jnp.zeros_like(gain_sum)
    pl.semaphore_wait(barrier, 3 * groups - 1)

    def remote(source, target, send, recv, there, other):
        return pltpu.make_async_remote_copy(
            src_ref=source,
            dst_ref=target,
            send_sem=send,
            recv_sem=recv,
            device_id={"section": there, "dp": other},
            device_id_type=MESH,
        )

    for source, target in weight_pieces(1 - core):
        remote(source, target, w_sem.at[0], w_sem.at[1], section, sibling).start()

    def far_z(i):
        away = jnp.where(i == 3, 0, jnp.where(i == 0, 2, 2 * i - 1))
        return lax.rem(z_pos + away, z_count)

    def far_device(i):
        x = lax.rem(x_pos + 1 - lax.rem(lax.div(i, 2), 2), 2)
        return far_z(lax.div(i, 4)) * 4 + x * 2 + lax.rem(core + 1 - lax.rem(i, 2), 2)

    def far_chip(i):
        return far_z(lax.div(i, 2)) * 2 + lax.rem(x_pos + 1 - lax.rem(i, 2), 2)

    def await_bytes(ref, sem):
        pltpu.make_async_copy(ref, ref, sem).wait()

    def row_mean(value):
        total = jnp.broadcast_to(jnp.sum(value, axis=-1, keepdims=True), (seg_rows, 128))
        return ((total + turned(total)) / width)[:, :1]

    def turned_place(m):
        wide = 2 * rows
        return (
            pl.ds(pl.multiple_of(core * half, half), half),
            pl.ds(pl.multiple_of(m * wide, wide), wide),
        )

    def keep_share(m):
        return remote(
            xturned.at[m],
            normed_out.at[turned_place(m)],
            keep_send.at[m],
            keep_recv.at[m],
            section,
            sibling,
        )

    def keep_own(m):
        return pltpu.make_async_copy(xturned.at[m], normed_out.at[turned_place(m)], keep_sem.at[m])

    def turn_normed(m):
        for q in range(quarter):
            sides = [[], []]
            for chain in range(2):
                one, two = (
                    gbuf[2 * m + u, chain, :, :, part(q)].astype(F32)
                    for u in range(2)
                )
                for h, whole in enumerate(unpack(one, two)):
                    sides[h].append(whole.reshape(rows, own_cols))
            for h in range(2):
                piece = jnp.transpose(jnp.concatenate(sides[h], axis=0))
                xturned[m, columns(q, h), :] = piece.astype(BF16)
        keep_share(m).start()
        keep_own(m).start()

    def slope_copy(m, chain):
        return pltpu.make_async_copy(
            own_slope.at[m, chain],
            slope_out.at[pl.ds(pl.multiple_of((m * 2 + chain) * rows, rows), rows), :],
            copy_sem.at[m, chain],
        )

    def send_shares(e):
        def send(step, carry):
            other = far_device(step)
            remote(
                slopes.at[1, e, lax.div(other, 2)],
                slope_in.at[e, core, chip],
                slope_send.at[1, e],
                slope_recv.at[e, core],
                section,
                other,
            ).start()
            return carry

        lax.fori_loop(0, groups - 1, send, 0)
        pltpu.make_async_copy(
            slopes.at[1, e, chip], slope_in.at[e, core, chip], slope_recv.at[e, core]
        ).start()

    @pl.when(last)
    def _():
        def share(e, carry):
            for q in range(chips):
                slopes[1, e, q] = cotangent_p[e, :, part(q)]
            send_shares(e)
            return carry

        lax.fori_loop(0, sets, share, 0)

    def pair_copy(e, chain):
        return remote(
            pout.at[e, chain],
            pair_in.at[e, chain],
            part_send.at[e, chain],
            pair_recv.at[e, chain],
            section,
            sibling,
        )

    def forward_rows(e):
        @pl.when(first & (e == 0) & (core == 1))
        def _():
            pl.semaphore_wait(stagger, 1)

        @pl.when(first)
        def _():
            incoming[...] = acts_p[e]

        @pl.when(jnp.logical_not(first))
        def _():
            await_bytes(arr_in.at[e], side_recv.at[0, e])
            await_bytes(pin.at[e], part_recv.at[e])
            for q in range(chips):
                value = pin[e, 2 * q].astype(F32) + pin[e, 2 * q + 1].astype(F32)
                hidden[e, :, part(q)] = value
                total = arr_in[e, :, part(q)].astype(F32) + gelu_value(value)
                incoming[:, part(q)] = total.astype(BF16).astype(F32)

        previous = before_p[e]
        moved = jnp.clip(incoming[...] - previous, -clip_limit, clip_limit)
        arrived_now = (previous + moved).astype(BF16)
        arrived[e] = arrived_now
        arrived_f = arrived_now.astype(F32)
        scale = lax.rsqrt(row_mean(arrived_f * arrived_f) + epsilon)
        scales[e] = jnp.broadcast_to(scale, (seg_rows, 128))
        normed = (arrived_f * scale * gains_p[...]).astype(BF16)
        for side in range(2):
            nbuf[e, side] = normed[:, side * fold : (side + 1) * fold]
        for p, (low_end, high_end) in enumerate(gather_parts):
            cut = slice(low_end, high_end)

            def send(step, carry, p=p, cut=cut):
                other = far_device(step)
                remote(
                    nbuf.at[e, lax.rem(other, 2), :, cut],
                    gbuf.at[e, core, chip, :, cut],
                    gather_send.at[e],
                    gather_recv.at[e, core, p],
                    section,
                    other,
                ).start()
                return carry

            lax.fori_loop(0, groups - 1, send, 0, unroll=True)
            pltpu.make_async_copy(
                nbuf.at[e, core, :, cut],
                gbuf.at[e, core, chip, :, cut],
                gather_recv.at[e, core, p],
            ).start()

        @pl.when(jnp.logical_not(last))
        def _():
            remote(
                arrived.at[e], arr_in.at[e], side_send.at[0, e], side_recv.at[0, e], after, me
            ).start()

        @pl.when(jnp.logical_not(first))
        def _():
            for q in range(chips):
                hidden[e, :, part(q)] = gelu_slope(hidden[e, :, part(q)])

    def forward_columns(e, chain):
        @pl.when((e == 0) & (chain == 0))
        def _():
            await_bytes(wbuf.at[:, :, own_place], w_sem.at[2])
            await_bytes(wbuf.at[:, :, own_place], w_sem.at[1])

        for p, (base, high_end) in enumerate(gather_parts):
            await_bytes(gbuf.at[e, chain, :, :, base:high_end], gather_recv.at[e, chain, p])
            if p == 0:

                @pl.when(first & (e == 0) & (chain == 0) & (core == 0))
                def _():
                    pl.semaphore_signal(
                        stagger, inc=1, device_id={"dp": sibling}, device_id_type=MESH
                    )

            piece = gbuf[e, chain, :, :, base:high_end].astype(F32)
            xbuf[:, base:high_end] = piece.reshape(rows, high_end - base).astype(BF16)
            for h in range(2):
                for c in range(0, chip_cols, 256):
                    product = jnp.dot(
                        xbuf[:, base:high_end],
                        wbuf[h, base:high_end, c : c + 256],
                        preferred_element_type=F32,
                    )
                    if p > 0:
                        product = product + products[h, :, c : c + 256]
                    products[h, :, c : c + 256] = product
        shape = (chips, seg_rows, own_cols)
        left = products[0, :, :own_cols].reshape(shape) + turned(
            products[1, :, :own_cols].reshape(shape)
        )
        right = (
            turned(products[0, :, own_cols:].reshape(shape))
            + products[1, :, own_cols:].reshape(shape)
        )
        pout[e, chain] = jnp.where(low_rows(shape), left, right).astype(BF16)

        def send(step, carry):
            q = far_chip(step)
            other = 2 * q + chain

            remote(
                pout.at[e, chain, q],
                pin.at[e, me],
                part_send.at[e, chain],
                part_recv.at[e],
                after,
                other,
            ).start()
            return carry

        @pl.when(jnp.logical_not(last))
        def _():
            lax.fori_loop(0, chips, send, 0, unroll=True)

        @pl.when(last)
        def _():
            pair_copy(e, chain).start()

    def backward_columns(e, chain):
        await_bytes(slope_in.at[e, chain], slope_recv.at[e, chain])

        @pl.when(last)
        def _():
            pair_copy(e, chain).wait_recv()
            value = pout[e, chain].astype(F32) + pair_in[e, chain].astype(F32)
            slope = slope_in[e, chain].astype(F32) * gelu_slope(value)
            slope_in[e, chain] = slope.astype(BF16)

        ybuf[...] = slope_in[e, chain].astype(F32).reshape(rows, own_cols).astype(BF16)
        for p, (low_end, high_end) in enumerate(back_parts):
            for start in range(low_end, high_end, step_b):
                shape = (chips, seg_rows, step_b)
                terms = [
                    [
                        lax.dot_general(
                            ybuf[...],
                            wbuf[h, start : start + step_b, s * own_cols : (s + 1) * own_cols],
                            (((1,), (1,)), ((), ())),
                            preferred_element_type=F32,
                        ).reshape(shape)
                        for s in range(2)
                    ]
                    for h in range(2)
                ]
                left = terms[0][0] + turned(terms[0][1])
                right = turned(terms[1][0]) + terms[1][1]
                back_out[e, chain, :, :, start : start + step_b] = jnp.where(
                    low_rows(shape), left, right
                ).astype(BF16)

            cut = slice(low_end, high_end)

            def send(step, carry, p=p, cut=cut):
                q = far_chip(step)
                other = 2 * q + chain

                @pl.when(other != me)
                def _():
                    remote(
                        back_out.at[e, chain, q, :, cut],
                        back_in.at[e, me, :, cut],
                        back_send.at[e, chain],
                        back_recv.at[e, p],
                        section,
                        other,
                    ).start()

                return carry

            @pl.when(jnp.logical_not(first))
            def _(p=p, send=send):
                lax.fori_loop(0, chips, send, 0, unroll=True)

            @pl.when(jnp.logical_not(first) & (core == chain))
            def _(p=p, cut=cut):
                pltpu.make_async_copy(
                    back_out.at[e, chain, chip, :, cut],
                    back_in.at[e, me, :, cut],
                    back_recv.at[e, p],
                ).start()

        for start in range(0, fold, 512):
            cut = slice(start, start + 512)
            term = back_out[e, chain, :, :, cut].astype(F32) * gbuf[e, chain, :, :, cut].astype(F32)
            gain_sum[:, cut] += jnp.sum(term, axis=0)

        @pl.when(lax.rem(e, 2) == 1)
        def _():
            m = lax.div(e, 2)
            left, right = unpack(
                slope_in[e - 1, chain].astype(F32), slope_in[e, chain].astype(F32)
            )
            mine = jnp.where(core == 0, left, right).reshape(rows, own_cols)
            own_slope[m, chain] = mine.astype(BF16)
            slope_copy(m, chain).start()

    def backward_rows(e):
        @pl.when(last)
        def _():
            up_in[e] = cotangent_p[e]

        @pl.when(jnp.logical_not(last))
        def _():
            await_bytes(up_in.at[e], side_recv.at[1, e])

        for p, (low_end, high_end) in enumerate(back_parts):
            cut = slice(low_end, high_end)
            await_bytes(back_in.at[e, :, :, cut], back_recv.at[e, p])
            for side in range(2):
                total = back_in[e, side, :, cut].astype(F32)
                for q in range(1, chips):
                    total = total + back_in[e, 2 * q + side, :, cut].astype(F32)
                incoming[:, side * fold + low_end : side * fold + high_end] = total
        back = incoming[...]
        arrived_f = arrived[e].astype(F32)
        scale = scales[e][:, :1]
        weighted = back * gains_p[...]
        mean_term = row_mean(weighted * arrived_f)
        total = up_in[e].astype(F32) + scale * (weighted - arrived_f * scale * scale * mean_term)
        up_out[e] = total.astype(BF16)

        def send(step, carry):
            q = far_chip(step)
            place = pl.ds(pl.multiple_of(q * own_cols, 128), own_cols)
            slope = up_out[e, :, place].astype(F32) * hidden[e, :, place]
            slopes[0, e, q] = slope.astype(BF16)
            for c in range(2):
                remote(
                    slopes.at[0, e, q],
                    slope_in.at[e, core, chip],
                    slope_send.at[0, e],
                    slope_recv.at[e, core],
                    before,
                    2 * q + c,
                ).start()
            return carry

        lax.fori_loop(0, chips, send, 0, unroll=True)

        @pl.when(section > 1)
        def _():
            remote(
                up_out.at[e], up_in.at[e], side_send.at[1, e], side_recv.at[1, e], before, me
            ).start()

    FR, FC, BC, BR, TN, NO = range(6)
    orders = [[make_order(micro, where, side) for side in range(2)] for where in range(2)]
    length = max(len(order) for pair in orders for order in pair)
    for pair in orders:
        for order in pair:
            order += [NO * 8] * (length - len(order))

    def run(t, carry):
        now = NO * 8
        for i in range(length):
            here = jnp.where(
                last,
                jnp.where(core == 0, orders[1][0][i], orders[1][1][i]),
                jnp.where(core == 0, orders[0][0][i], orders[0][1][i]),
            )
            now = jnp.where(t == i, here, now)
        kind = lax.div(now, 8)
        e = lax.rem(lax.div(now, 2), sets)
        chain = lax.rem(now, 2)
        pl.when(kind == FR)(lambda: forward_rows(e))
        pl.when(kind == FC)(lambda: forward_columns(e, chain))
        pl.when(kind == BC)(lambda: backward_columns(e, chain))
        pl.when((kind == BR) & jnp.logical_not(first))(lambda: backward_rows(e))
        pl.when(kind == TN)(lambda: turn_normed(lax.div(e, 2)))
        return carry

    lax.fori_loop(0, length, run, 0)

    low = low_rows(gain_sum.shape)
    sums = gain_sum[...]
    left = jnp.sum(jnp.where(low, sums, 0.0), axis=0, keepdims=True)
    right = jnp.sum(jnp.where(low, 0.0, sums), axis=0, keepdims=True)
    own_gains = jnp.where(core == 0, gains[:, :half], gains[:, half:])
    for q in range(quarter):
        for h, value in enumerate((left, right)):
            gain_row[:, columns(q, h)] = value[:, part(q)] / own_gains[:, columns(q, h)]

    def gain_send(step, carry):
        other = far_device(step)
        remote(
            gain_row, gain_in.at[me], gain_sem.at[0], gain_sem.at[1], section, other
        ).start()
        return carry

    lax.fori_loop(0, groups - 1, gain_send, 0)
    pltpu.make_async_copy(gain_row, gain_in.at[me], gain_sem.at[1]).start()

    for m in range(micro):
        for q in range(chips):
            wholes = unpack(
                arrived[2 * m, :, part(q)].astype(F32), arrived[2 * m + 1, :, part(q)].astype(F32)
            )
            for h, whole in enumerate(wholes):
                arrived_whole[m, :, columns(q, h)] = whole.astype(BF16)
    arrived_copy = pltpu.make_async_copy(arrived_whole, arrived_out, gain_sem.at[2])
    arrived_copy.start()
    await_bytes(wbuf.at[:, :, own_place], w_sem.at[0])
    for e in range(sets):
        await_bytes(back_in.at[e, 0 : groups - 1], gather_send.at[e])
        for chain in range(2):
            await_bytes(pout.at[e, chain], part_send.at[e, chain])

            @pl.when(jnp.logical_not(first) & (core == chain))
            def _(e=e, chain=chain):
                await_bytes(back_out.at[e, chain, 0 : chips - 1], back_send.at[e, chain])

            @pl.when(jnp.logical_not(first) & (core != chain))
            def _(e=e, chain=chain):
                await_bytes(back_out.at[e, chain], back_send.at[e, chain])

        @pl.when(last)
        def _(e=e):
            await_bytes(pin.at[e, 0 : groups - 1], slope_send.at[1, e])

        @pl.when(jnp.logical_not(first))
        def _(e=e):
            await_bytes(pin.at[e], slope_send.at[0, e])

        @pl.when(section > 1)
        def _(e=e):
            await_bytes(up_out.at[e], side_send.at[1, e])

        @pl.when(jnp.logical_not(last))
        def _(e=e):
            await_bytes(arrived.at[e], side_send.at[0, e])

    for m in range(micro):
        for chain in range(2):
            slope_copy(m, chain).wait()
        keep_share(m).wait()
        keep_own(m).wait()

    await_bytes(gain_in, gain_sem.at[1])
    for side in range(2):
        total = gain_in[side]
        for q in range(1, chips):
            total = total + gain_in[2 * q + side]
        gain_full[:, side * half : (side + 1) * half] = total
    await_bytes(gain_in.at[0 : groups - 1], gain_sem.at[0])
    gain_copy = pltpu.make_async_copy(gain_full, gain_out, gain_sem.at[3])
    gain_copy.start()
    arrived_copy.wait()
    gain_copy.wait()


def on_device(sections, groups, acts_in, weights, gains, stored, sample_ids, cotangent):
    micro, seg_rows, width = acts_in.shape
    own_cols = weights.shape[2]
    half = width // 2
    fold = half // 2
    chip_cols = 2 * own_cols
    chips = groups // 2
    rows = chips * seg_rows
    sets = 2 * micro
    flat_ids = sample_ids.reshape(micro)
    anywhere = pl.BlockSpec(memory_space=pl.ANY)
    smem = pl.BlockSpec(memory_space=pltpu.SMEM)
    dma = pltpu.SemaphoreType.DMA
    arrived, normed, slope, gain = pl.pallas_call(
        functools.partial(relay, sections, groups),
        out_shape=(
            jax.ShapeDtypeStruct((micro, seg_rows, width), BF16),
            jax.ShapeDtypeStruct((width, micro * 2 * rows), BF16),
            jax.ShapeDtypeStruct((micro * 2 * rows, own_cols), BF16),
            jax.ShapeDtypeStruct((1, width), F32),
        ),
        in_specs=[smem] + [anywhere] * 5,
        out_specs=(anywhere,) * 4,
        scratch_shapes=[
            pltpu.VMEM((micro, seg_rows, width), BF16),
            pltpu.VMEM((1, width), F32),
            pltpu.VMEM(stored.shape, BF16),
            pltpu.VMEM((micro, seg_rows, width), BF16),
            pltpu.VMEM((sets, seg_rows, half), F32),
            pltpu.VMEM((sets, seg_rows, half), F32),
            pltpu.VMEM((sets, seg_rows, half), BF16),
            pltpu.VMEM((seg_rows, half), F32),
            pltpu.VMEM((2, fold, chip_cols), BF16),
            pltpu.VMEM((sets, 2, seg_rows, fold), BF16),
            pltpu.VMEM((sets, 2, chips, seg_rows, fold), BF16),
            pltpu.VMEM((rows, fold), BF16),
            pltpu.VMEM((2, rows, chip_cols), F32),
            pltpu.VMEM((sets, 2, chips, seg_rows, own_cols), BF16),
            pltpu.VMEM((sets, groups, seg_rows, own_cols), BF16),
            pltpu.VMEM((sets, 2, chips, seg_rows, own_cols), BF16),
            pltpu.VMEM((sets, seg_rows, half), F32),
            pltpu.VMEM((seg_rows, half), F32),
            pltpu.VMEM((sets, seg_rows, half), BF16),
            pltpu.VMEM((micro, seg_rows, width), BF16),
            pltpu.VMEM((sets, seg_rows, half), BF16),
            pltpu.VMEM((2, sets, chips, seg_rows, own_cols), BF16),
            pltpu.VMEM((sets, 2, chips, seg_rows, own_cols), BF16),
            pltpu.VMEM((rows, own_cols), BF16),
            pltpu.VMEM((micro, 2, rows, own_cols), BF16),
            pltpu.VMEM((sets, 2, chips, seg_rows, fold), BF16),
            pltpu.VMEM((sets, groups, seg_rows, fold), BF16),
            pltpu.VMEM((sets, seg_rows, half), BF16),
            pltpu.VMEM((sets, seg_rows, half), BF16),
            pltpu.VMEM((sets, seg_rows, 128), F32),
            pltpu.VMEM((micro, half, 2 * rows), BF16),
            pltpu.VMEM((seg_rows, fold), F32),
            pltpu.VMEM((1, half), F32),
            pltpu.VMEM((groups, 1, half), F32),
            pltpu.VMEM((1, width), F32),
            dma((4,)),
            dma((3,)),
            dma((sets,)),
            dma((sets, 2, len(gather_cuts) - 1)),
            dma((sets, 2)),
            dma((sets,)),
            dma((sets, 2)),
            dma((2, sets)),
            dma((sets, 2)),
            dma((sets, 2)),
            dma((sets, len(back_cuts) - 1)),
            dma((2, sets)),
            dma((2, sets)),
            dma((micro,)),
            dma((micro,)),
            dma((micro,)),
            dma((micro, 2)),
            dma((4,)),
            pltpu.SemaphoreType.REGULAR,
        ],
        compiler_params=pltpu.CompilerParams(
            collective_id=0, has_side_effects=True, vmem_limit_bytes=60 * 1024 * 1024
        ),
    )(flat_ids, acts_in, weights, gains, stored, cotangent)

    block_k = 1536
    blocks = width // block_k
    slot_count = stored.shape[1]

    def finish(
        ids_ref, normed_ref, slope_ref, stored_ref, arrived_ref, gain_ref,
        kept_ref, grad_ref, total_ref,
        normed_buf, slope_buf, kept_buf, arrived_buf, grad_buf, in_sem, out_sem, side_sem,
    ):
        side = [
            pltpu.make_async_copy(slope_ref, slope_buf, side_sem.at[0]),
            pltpu.make_async_copy(stored_ref, kept_buf, side_sem.at[1]),
            pltpu.make_async_copy(arrived_ref, arrived_buf, side_sem.at[2]),
            pltpu.make_async_copy(gain_ref, total_ref, side_sem.at[3]),
        ]
        places = [pl.ds(b * block_k, block_k) for b in range(blocks)]
        takes = [
            pltpu.make_async_copy(normed_ref.at[place], normed_buf.at[place], in_sem.at[b])
            for b, place in enumerate(places)
        ]
        gives = [
            pltpu.make_async_copy(grad_buf.at[place], grad_ref.at[0, place], out_sem.at[b])
            for b, place in enumerate(places)
        ]
        side[0].start()
        for take in takes:
            take.start()
        for copy in side[1:]:
            copy.start()
        side[0].wait()
        for place, take, give in zip(places, takes, gives):
            take.wait()
            grad_buf[place] = jnp.dot(
                normed_buf[place], slope_buf[...], preferred_element_type=F32
            )
            give.start()
        side[1].wait()
        side[2].wait()
        for m in range(micro):
            slot = ids_ref[m] - lax.axis_index("dp") * slot_count
            kept_buf[0, jnp.clip(slot, 0, slot_count - 1)] = arrived_buf[m]
        kept_copy = pltpu.make_async_copy(kept_buf, kept_ref, side_sem.at[4])
        kept_copy.start()
        side[3].wait()
        kept_copy.wait()
        for give in gives:
            give.wait()

    kept, grad, gain = pl.pallas_call(
        finish,
        out_shape=(
            jax.ShapeDtypeStruct(stored.shape, BF16),
            jax.ShapeDtypeStruct((1, width, own_cols), F32),
            jax.ShapeDtypeStruct((1, width), F32),
        ),
        in_specs=[smem] + [anywhere] * 5,
        out_specs=(anywhere,) * 3,
        scratch_shapes=[
            pltpu.VMEM(normed.shape, BF16),
            pltpu.VMEM(slope.shape, BF16),
            pltpu.VMEM(stored.shape, BF16),
            pltpu.VMEM(arrived.shape, BF16),
            pltpu.VMEM((width, own_cols), F32),
            dma((blocks,)),
            dma((blocks,)),
            dma((5,)),
        ],
        compiler_params=pltpu.CompilerParams(vmem_limit_bytes=60 * 1024 * 1024),
    )(flat_ids, normed, slope, stored, arrived, gain)
    return (kept, grad, gain)


def solution(mesh):
    placed = (
        P(None, "dp", None),
        P("section", None, "dp"),
        P("section", None),
        P("section", "dp", None, None),
        P(None, "dp"),
        P(None, "dp", None),
    )
    return jax.shard_map(
        functools.partial(on_device, mesh.shape["section"], mesh.shape["dp"]),
        mesh=mesh,
        in_specs=placed,
        out_specs=(P("section", "dp", None, None), P("section", None, "dp"), P("section", None)),
        check_vma=False,
    )
```

```python
import functools

import jax
import jax.numpy as jnp
from jax import lax
from jax.experimental import pallas as pl
from jax.experimental.pallas import tpu as pltpu
from jax.sharding import PartitionSpec as P

MESH = pl.DeviceIdType.MESH
F32 = jnp.float32
BF16 = jnp.bfloat16

clip_limit = 1.0
epsilon = 1e-05
gelu_coeff = 0.7978845608028654


def gelu_value(values):
    inner = gelu_coeff * (values + 0.044715 * values * values * values)
    return 0.5 * values * (1.0 + jnp.tanh(inner))


def gelu_slope(values):
    tangent = jnp.tanh(gelu_coeff * (values + 0.044715 * values * values * values))
    return 0.5 * (1.0 + tangent) + 0.5 * values * (1.0 - tangent * tangent) * gelu_coeff * (
        1.0 + 0.134145 * values * values
    )


gather_cuts = (0, 768, 1280, 1536)
back_cuts = (0, 512, 1024, 1536)
step_b = 256
plain_us = (3.5, 5.5, 2.8, 6.4, 0.0)
turning_us = (3.5, 5.5, 1.4, 6.4, 0.0)


def make_order(micro, turning, side):
    FR, FC, BC, BR, TN = range(5)
    stagger_us, gather_us, pair_us, back_us, late_us = turning_us if turning else plain_us
    events = []
    for k in range(4 * micro):
        start = stagger_us * k
        back = start + gather_us + pair_us if turning else start + 1000.0
        events.append((start + gather_us, FC * 8 + k))
        events.append((back, BC * 8 + k))
        if k % 2 == side:
            events.append((start + (late_us if k >= 4 else 0.0), FR * 8 + k))
            events.append((back + back_us, BR * 8 + k))
    for m in range(micro):
        events.append((2000.0 if turning else 500.0, TN * 8 + 4 * m))
    return [entry for _, entry in sorted(events)]


def relay(
    sections,
    groups,
    ids,
    acts_hbm,
    weights,
    gains_hbm,
    stored_hbm,
    cotangent_hbm,
    arrived_out,
    normed_out,
    slope_out,
    gain_out,
    acts,
    gains,
    stored,
    cotangent,
    acts_p,
    before_p,
    cotangent_p,
    gains_p,
    wbuf,
    nbuf,
    gbuf,
    xbuf,
    products,
    pout,
    pin,
    pair_in,
    hidden,
    incoming,
    arrived,
    arrived_whole,
    arr_in,
    slopes,
    slope_in,
    ybuf,
    own_slope,
    back_out,
    back_in,
    up_in,
    up_out,
    scales,
    xturned,
    gain_sum,
    gain_row,
    gain_in,
    gain_full,
    load_sem,
    w_sem,
    gather_send,
    gather_recv,
    part_send,
    part_recv,
    pair_recv,
    slope_send,
    slope_recv,
    back_send,
    back_recv,
    side_send,
    side_recv,
    keep_send,
    keep_recv,
    keep_sem,
    copy_sem,
    gain_sem,
    stagger,
):
    micro, seg_rows, width = acts.shape
    half = width // 2
    fold = half // 2
    own_cols = weights.shape[2]
    chip_cols = 2 * own_cols
    chips = groups // 2
    quarter = chips // 2
    rows = chips * seg_rows
    slot_count = stored.shape[1]
    sets = 2 * micro
    gather_parts = list(zip(gather_cuts[:-1], gather_cuts[1:]))
    back_parts = list(zip(back_cuts[:-1], back_cuts[1:]))
    section = lax.axis_index("section")
    me = lax.axis_index("dp")
    core = lax.rem(me, 2)
    chip = lax.div(me, 2)
    sibling = me + 1 - 2 * core
    first = section == 0
    last = section == sections - 1
    after = lax.rem(section + 1, sections)
    before = lax.rem(section + sections - 1, sections)
    z_count = groups // 4
    z_pos = lax.div(me, 4)
    x_pos = lax.rem(chip, 2)

    barrier = pltpu.get_barrier_semaphore()

    def greet(step, carry):
        other = lax.rem(me + step, groups)
        for there in (after, before):
            pl.semaphore_signal(
                barrier, inc=1, device_id={"section": there, "dp": other}, device_id_type=MESH
            )

        @pl.when(step > 0)
        def _():
            pl.semaphore_signal(
                barrier, inc=1, device_id={"section": section, "dp": other}, device_id_type=MESH
            )

        return carry

    lax.fori_loop(0, groups, greet, 0, unroll=True)

    loads = [
        pltpu.make_async_copy(source, target, load_sem.at[i])
        for i, (source, target) in enumerate(
            (
                (acts_hbm, acts),
                (stored_hbm, stored),
                (gains_hbm, gains),
                (cotangent_hbm, cotangent),
            )
        )
    ]
    for load in loads:
        load.start()
    own_place = pl.ds(pl.multiple_of(core * own_cols, 128), own_cols)

    def weight_pieces(side):
        for q in range(quarter):
            for h in range(2):
                yield (
                    weights.at[
                        0, pl.ds(side * half + q * chip_cols + h * own_cols, own_cols), :
                    ],
                    wbuf.at[h, q * own_cols : (q + 1) * own_cols, own_place],
                )

    for source, target in weight_pieces(core):
        pltpu.make_async_copy(source, target, w_sem.at[2]).start()

    def part(q):
        return slice(q * own_cols, (q + 1) * own_cols)

    def low_rows(shape):
        return lax.broadcasted_iota(jnp.int32, shape, len(shape) - 2) < 4

    def turned(value):
        return pltpu.roll(value, 4, axis=value.ndim - 2)

    def columns(q, h):
        start = q * chip_cols + h * own_cols
        return slice(start, start + own_cols)

    def pack(value, target, index):
        for q in range(chips):
            left, right = value[:, columns(q, 0)], value[:, columns(q, 1)]
            low = low_rows(left.shape)
            target[index, :, part(q)] = jnp.where(low, left, turned(right)).astype(target.dtype)
            target[index + 1, :, part(q)] = jnp.where(low, turned(left), right).astype(
                target.dtype
            )

    def unpack(one, two):
        low = low_rows(one.shape)
        return jnp.where(low, one, turned(two)), jnp.where(low, turned(one), two)

    def double(packed):
        low, other = low_rows(packed.shape), turned(packed)
        return jnp.where(low, packed, other), jnp.where(low, other, packed)

    for load in loads:
        load.wait()
    for q in range(chips):
        left = jnp.broadcast_to(gains[:, columns(q, 0)], (seg_rows, own_cols))
        right = jnp.broadcast_to(gains[:, columns(q, 1)], (seg_rows, own_cols))
        gains_p[:, part(q)] = jnp.where(low_rows(left.shape), left, right)
    for m in range(micro):
        slot = jnp.clip(ids[m] - me * slot_count, 0, slot_count - 1)
        pack(acts[m].astype(F32), acts_p, 2 * m)
        pack(stored[0, slot].astype(F32), before_p, 2 * m)
        pack(cotangent[m].astype(F32), cotangent_p, 2 * m)
    gain_sum[...] = jnp.zeros_like(gain_sum)
    pl.semaphore_wait(barrier, 3 * groups - 1)

    def remote(source, target, send, recv, there, other):
        return pltpu.make_async_remote_copy(
            src_ref=source,
            dst_ref=target,
            send_sem=send,
            recv_sem=recv,
            device_id={"section": there, "dp": other},
            device_id_type=MESH,
        )

    for source, target in weight_pieces(1 - core):
        remote(source, target, w_sem.at[0], w_sem.at[1], section, sibling).start()

    def far_z(i):
        away = jnp.where(i == 3, 0, jnp.where(i == 0, 2, 2 * i - 1))
        return lax.rem(z_pos + away, z_count)

    def far_device(i):
        x = lax.rem(x_pos + 1 - lax.rem(lax.div(i, 2), 2), 2)
        return far_z(lax.div(i, 4)) * 4 + x * 2 + lax.rem(core + 1 - lax.rem(i, 2), 2)

    def far_chip(i):
        return far_z(lax.div(i, 2)) * 2 + lax.rem(x_pos + 1 - lax.rem(i, 2), 2)

    def await_bytes(ref, sem):
        pltpu.make_async_copy(ref, ref, sem).wait()

    def row_mean(value):
        total = jnp.broadcast_to(jnp.sum(value, axis=-1, keepdims=True), (seg_rows, 128))
        return ((total + turned(total)) / width)[:, :1]

    def turned_place(m):
        wide = 2 * rows
        return (
            pl.ds(pl.multiple_of(core * half, half), half),
            pl.ds(pl.multiple_of(m * wide, wide), wide),
        )

    def keep_share(m):
        return remote(
            xturned.at[m],
            normed_out.at[turned_place(m)],
            keep_send.at[m],
            keep_recv.at[m],
            section,
            sibling,
        )

    def keep_own(m):
        return pltpu.make_async_copy(xturned.at[m], normed_out.at[turned_place(m)], keep_sem.at[m])

    def turn_normed(m):
        for q in range(quarter):
            sides = [[], []]
            for chain in range(2):
                one, two = (
                    gbuf[2 * m + u, chain, :, :, part(q)].astype(F32)
                    for u in range(2)
                )
                for h, whole in enumerate(unpack(one, two)):
                    sides[h].append(whole.reshape(rows, own_cols))
            for h in range(2):
                piece = jnp.transpose(jnp.concatenate(sides[h], axis=0))
                xturned[m, columns(q, h), :] = piece.astype(BF16)
        keep_share(m).start()
        keep_own(m).start()

    def slope_copy(m, chain):
        return pltpu.make_async_copy(
            own_slope.at[m, chain],
            slope_out.at[pl.ds(pl.multiple_of((m * 2 + chain) * rows, rows), rows), :],
            copy_sem.at[m, chain],
        )

    def send_shares(e):
        def send(step, carry):
            other = far_device(step)
            remote(
                slopes.at[1, e, lax.div(other, 2)],
                slope_in.at[e, core, chip],
                slope_send.at[1, e],
                slope_recv.at[e, core],
                section,
                other,
            ).start()
            return carry

        lax.fori_loop(0, groups - 1, send, 0)
        pltpu.make_async_copy(
            slopes.at[1, e, chip], slope_in.at[e, core, chip], slope_recv.at[e, core]
        ).start()

    @pl.when(last)
    def _():
        def share(e, carry):
            for q in range(chips):
                slopes[1, e, q] = cotangent_p[e, :, part(q)]
            send_shares(e)
            return carry

        lax.fori_loop(0, sets, share, 0)

    def pair_copy(e, chain):
        return remote(
            pout.at[e, chain],
            pair_in.at[e, chain],
            part_send.at[e, chain],
            pair_recv.at[e, chain],
            section,
            sibling,
        )

    def forward_rows(e):
        @pl.when(first & (e == 0) & (core == 1))
        def _():
            pl.semaphore_wait(stagger, 1)

        @pl.when(first)
        def _():
            incoming[...] = acts_p[e]

        @pl.when(jnp.logical_not(first))
        def _():
            await_bytes(arr_in.at[e], side_recv.at[0, e])
            await_bytes(pin.at[e], part_recv.at[e])
            for q in range(chips):
                value = pin[e, 2 * q].astype(F32) + pin[e, 2 * q + 1].astype(F32)
                hidden[e, :, part(q)] = value
                total = arr_in[e, :, part(q)].astype(F32) + gelu_value(value)
                incoming[:, part(q)] = total.astype(BF16).astype(F32)

        previous = before_p[e]
        moved = jnp.clip(incoming[...] - previous, -clip_limit, clip_limit)
        arrived_now = (previous + moved).astype(BF16)
        arrived[e] = arrived_now
        arrived_f = arrived_now.astype(F32)
        scale = lax.rsqrt(row_mean(arrived_f * arrived_f) + epsilon)
        scales[e] = jnp.broadcast_to(scale, (seg_rows, 128))
        normed = (arrived_f * scale * gains_p[...]).astype(BF16)
        for side in range(2):
            nbuf[e, side] = normed[:, side * fold : (side + 1) * fold]
        for p, (low_end, high_end) in enumerate(gather_parts):
            cut = slice(low_end, high_end)

            def send(step, carry, p=p, cut=cut):
                other = far_device(step)
                remote(
                    nbuf.at[e, lax.rem(other, 2), :, cut],
                    gbuf.at[e, core, chip, :, cut],
                    gather_send.at[e],
                    gather_recv.at[e, core, p],
                    section,
                    other,
                ).start()
                return carry

            lax.fori_loop(0, groups - 1, send, 0, unroll=True)
            pltpu.make_async_copy(
                nbuf.at[e, core, :, cut],
                gbuf.at[e, core, chip, :, cut],
                gather_recv.at[e, core, p],
            ).start()

        @pl.when(jnp.logical_not(last))
        def _():
            remote(
                arrived.at[e], arr_in.at[e], side_send.at[0, e], side_recv.at[0, e], after, me
            ).start()

        @pl.when(jnp.logical_not(first))
        def _():
            for q in range(chips):
                hidden[e, :, part(q)] = gelu_slope(hidden[e, :, part(q)])

    def forward_columns(e, chain):
        @pl.when((e == 0) & (chain == 0))
        def _():
            await_bytes(wbuf.at[:, :, own_place], w_sem.at[2])
            await_bytes(wbuf.at[:, :, own_place], w_sem.at[1])

        for p, (base, high_end) in enumerate(gather_parts):
            await_bytes(gbuf.at[e, chain, :, :, base:high_end], gather_recv.at[e, chain, p])
            if p == 0:

                @pl.when(first & (e == 0) & (chain == 0) & (core == 0))
                def _():
                    pl.semaphore_signal(
                        stagger, inc=1, device_id={"dp": sibling}, device_id_type=MESH
                    )

            piece = gbuf[e, chain, :, :, base:high_end].astype(F32)
            for h, whole in enumerate(double(piece)):
                xbuf[h, :, base:high_end] = whole.reshape(rows, high_end - base).astype(BF16)
            for c in range(0, chip_cols, 256):
                product = sum(
                    jnp.dot(
                        xbuf[h, :, base:high_end],
                        wbuf[h, base:high_end, c : c + 256],
                        preferred_element_type=F32,
                    )
                    for h in range(2)
                )
                if p > 0:
                    product = product + products[:, c : c + 256]
                products[:, c : c + 256] = product
        shape = (chips, seg_rows, own_cols)
        pout[e, chain] = jnp.where(
            low_rows(shape),
            products[:, :own_cols].reshape(shape),
            products[:, own_cols:].reshape(shape),
        ).astype(BF16)

        def send(step, carry):
            q = far_chip(step)
            other = 2 * q + chain

            remote(
                pout.at[e, chain, q],
                pin.at[e, me],
                part_send.at[e, chain],
                part_recv.at[e],
                after,
                other,
            ).start()
            return carry

        @pl.when(jnp.logical_not(last))
        def _():
            lax.fori_loop(0, chips, send, 0, unroll=True)

        @pl.when(last)
        def _():
            pair_copy(e, chain).start()

    def backward_columns(e, chain):
        await_bytes(slope_in.at[e, chain], slope_recv.at[e, chain])

        @pl.when(last)
        def _():
            pair_copy(e, chain).wait_recv()
            value = pout[e, chain].astype(F32) + pair_in[e, chain].astype(F32)
            slope = slope_in[e, chain].astype(F32) * gelu_slope(value)
            slope_in[e, chain] = slope.astype(BF16)

        for s, whole in enumerate(double(slope_in[e, chain].astype(F32))):
            ybuf[:, part(s)] = whole.reshape(rows, own_cols).astype(BF16)
        for p, (low_end, high_end) in enumerate(back_parts):
            for start in range(low_end, high_end, step_b):
                shape = (chips, seg_rows, step_b)
                left, right = (
                    lax.dot_general(
                        ybuf[...],
                        wbuf[h, start : start + step_b, :],
                        (((1,), (1,)), ((), ())),
                        preferred_element_type=F32,
                    ).reshape(shape)
                    for h in range(2)
                )
                back_out[e, chain, :, :, start : start + step_b] = jnp.where(
                    low_rows(shape), left, right
                ).astype(BF16)

            cut = slice(low_end, high_end)

            def send(step, carry, p=p, cut=cut):
                q = far_chip(step)
                other = 2 * q + chain

                @pl.when(other != me)
                def _():
                    remote(
                        back_out.at[e, chain, q, :, cut],
                        back_in.at[e, me, :, cut],
                        back_send.at[e, chain],
                        back_recv.at[e, p],
                        section,
                        other,
                    ).start()

                return carry

            @pl.when(jnp.logical_not(first))
            def _(p=p, send=send):
                lax.fori_loop(0, chips, send, 0, unroll=True)

            @pl.when(jnp.logical_not(first) & (core == chain))
            def _(p=p, cut=cut):
                pltpu.make_async_copy(
                    back_out.at[e, chain, chip, :, cut],
                    back_in.at[e, me, :, cut],
                    back_recv.at[e, p],
                ).start()

        for start in range(0, fold, 512):
            cut = slice(start, start + 512)
            term = back_out[e, chain, :, :, cut].astype(F32) * gbuf[e, chain, :, :, cut].astype(F32)
            gain_sum[:, cut] += jnp.sum(term, axis=0)

        @pl.when(lax.rem(e, 2) == 1)
        def _():
            m = lax.div(e, 2)
            left, right = unpack(
                slope_in[e - 1, chain].astype(F32), slope_in[e, chain].astype(F32)
            )
            mine = jnp.where(core == 0, left, right).reshape(rows, own_cols)
            own_slope[m, chain] = mine.astype(BF16)
            slope_copy(m, chain).start()

    def backward_rows(e):
        @pl.when(last)
        def _():
            up_in[e] = cotangent_p[e]

        @pl.when(jnp.logical_not(last))
        def _():
            await_bytes(up_in.at[e], side_recv.at[1, e])

        for p, (low_end, high_end) in enumerate(back_parts):
            cut = slice(low_end, high_end)
            await_bytes(back_in.at[e, :, :, cut], back_recv.at[e, p])
            for side in range(2):
                total = back_in[e, side, :, cut].astype(F32)
                for q in range(1, chips):
                    total = total + back_in[e, 2 * q + side, :, cut].astype(F32)
                incoming[:, side * fold + low_end : side * fold + high_end] = total
        back = incoming[...]
        arrived_f = arrived[e].astype(F32)
        scale = scales[e][:, :1]
        weighted = back * gains_p[...]
        mean_term = row_mean(weighted * arrived_f)
        total = up_in[e].astype(F32) + scale * (weighted - arrived_f * scale * scale * mean_term)
        up_out[e] = total.astype(BF16)

        def send(step, carry):
            q = far_chip(step)
            place = pl.ds(pl.multiple_of(q * own_cols, 128), own_cols)
            slope = up_out[e, :, place].astype(F32) * hidden[e, :, place]
            slopes[0, e, q] = slope.astype(BF16)
            for c in range(2):
                remote(
                    slopes.at[0, e, q],
                    slope_in.at[e, core, chip],
                    slope_send.at[0, e],
                    slope_recv.at[e, core],
                    before,
                    2 * q + c,
                ).start()
            return carry

        lax.fori_loop(0, chips, send, 0, unroll=True)

        @pl.when(section > 1)
        def _():
            remote(
                up_out.at[e], up_in.at[e], side_send.at[1, e], side_recv.at[1, e], before, me
            ).start()

    FR, FC, BC, BR, TN, NO = range(6)
    orders = [[make_order(micro, where, side) for side in range(2)] for where in range(2)]
    length = max(len(order) for pair in orders for order in pair)
    for pair in orders:
        for order in pair:
            order += [NO * 8] * (length - len(order))

    def run(t, carry):
        now = NO * 8
        for i in range(length):
            here = jnp.where(
                last,
                jnp.where(core == 0, orders[1][0][i], orders[1][1][i]),
                jnp.where(core == 0, orders[0][0][i], orders[0][1][i]),
            )
            now = jnp.where(t == i, here, now)
        kind = lax.div(now, 8)
        e = lax.rem(lax.div(now, 2), sets)
        chain = lax.rem(now, 2)
        pl.when(kind == FR)(lambda: forward_rows(e))
        pl.when(kind == FC)(lambda: forward_columns(e, chain))
        pl.when(kind == BC)(lambda: backward_columns(e, chain))
        pl.when((kind == BR) & jnp.logical_not(first))(lambda: backward_rows(e))
        pl.when(kind == TN)(lambda: turn_normed(lax.div(e, 2)))
        return carry

    lax.fori_loop(0, length, run, 0)

    low = low_rows(gain_sum.shape)
    sums = gain_sum[...]
    left = jnp.sum(jnp.where(low, sums, 0.0), axis=0, keepdims=True)
    right = jnp.sum(jnp.where(low, 0.0, sums), axis=0, keepdims=True)
    own_gains = jnp.where(core == 0, gains[:, :half], gains[:, half:])
    for q in range(quarter):
        for h, value in enumerate((left, right)):
            gain_row[:, columns(q, h)] = value[:, part(q)] / own_gains[:, columns(q, h)]

    def gain_send(step, carry):
        other = far_device(step)
        remote(
            gain_row, gain_in.at[me], gain_sem.at[0], gain_sem.at[1], section, other
        ).start()
        return carry

    lax.fori_loop(0, groups - 1, gain_send, 0, unroll=True)
    pltpu.make_async_copy(gain_row, gain_in.at[me], gain_sem.at[1]).start()

    for m in range(micro):
        for q in range(chips):
            wholes = unpack(
                arrived[2 * m, :, part(q)].astype(F32), arrived[2 * m + 1, :, part(q)].astype(F32)
            )
            for h, whole in enumerate(wholes):
                arrived_whole[m, :, columns(q, h)] = whole.astype(BF16)
    arrived_copy = pltpu.make_async_copy(arrived_whole, arrived_out, gain_sem.at[2])
    arrived_copy.start()
    await_bytes(wbuf.at[:, :, own_place], w_sem.at[0])
    for e in range(sets):
        await_bytes(back_in.at[e, 0 : groups - 1], gather_send.at[e])
        for chain in range(2):
            await_bytes(pout.at[e, chain], part_send.at[e, chain])

            @pl.when(jnp.logical_not(first) & (core == chain))
            def _(e=e, chain=chain):
                await_bytes(back_out.at[e, chain, 0 : chips - 1], back_send.at[e, chain])

            @pl.when(jnp.logical_not(first) & (core != chain))
            def _(e=e, chain=chain):
                await_bytes(back_out.at[e, chain], back_send.at[e, chain])

        @pl.when(last)
        def _(e=e):
            await_bytes(pin.at[e, 0 : groups - 1], slope_send.at[1, e])

        @pl.when(jnp.logical_not(first))
        def _(e=e):
            await_bytes(pin.at[e], slope_send.at[0, e])

        @pl.when(section > 1)
        def _(e=e):
            await_bytes(up_out.at[e], side_send.at[1, e])

        @pl.when(jnp.logical_not(last))
        def _(e=e):
            await_bytes(arrived.at[e], side_send.at[0, e])

    for m in range(micro):
        for chain in range(2):
            slope_copy(m, chain).wait()
        keep_share(m).wait()
        keep_own(m).wait()

    await_bytes(gain_in, gain_sem.at[1])
    for side in range(2):
        total = gain_in[side]
        for q in range(1, chips):
            total = total + gain_in[2 * q + side]
        gain_full[:, side * half : (side + 1) * half] = total
    await_bytes(gain_in.at[0 : groups - 1], gain_sem.at[0])
    gain_copy = pltpu.make_async_copy(gain_full, gain_out, gain_sem.at[3])
    gain_copy.start()
    arrived_copy.wait()
    gain_copy.wait()


def on_device(sections, groups, acts_in, weights, gains, stored, sample_ids, cotangent):
    micro, seg_rows, width = acts_in.shape
    own_cols = weights.shape[2]
    half = width // 2
    fold = half // 2
    chip_cols = 2 * own_cols
    chips = groups // 2
    rows = chips * seg_rows
    sets = 2 * micro
    flat_ids = sample_ids.reshape(micro)
    anywhere = pl.BlockSpec(memory_space=pl.ANY)
    smem = pl.BlockSpec(memory_space=pltpu.SMEM)
    dma = pltpu.SemaphoreType.DMA
    arrived, normed, slope, gain = pl.pallas_call(
        functools.partial(relay, sections, groups),
        out_shape=(
            jax.ShapeDtypeStruct((micro, seg_rows, width), BF16),
            jax.ShapeDtypeStruct((width, micro * 2 * rows), BF16),
            jax.ShapeDtypeStruct((micro * 2 * rows, own_cols), BF16),
            jax.ShapeDtypeStruct((1, width), F32),
        ),
        in_specs=[smem] + [anywhere] * 5,
        out_specs=(anywhere,) * 4,
        scratch_shapes=[
            pltpu.VMEM((micro, seg_rows, width), BF16),
            pltpu.VMEM((1, width), F32),
            pltpu.VMEM(stored.shape, BF16),
            pltpu.VMEM((micro, seg_rows, width), BF16),
            pltpu.VMEM((sets, seg_rows, half), F32),
            pltpu.VMEM((sets, seg_rows, half), F32),
            pltpu.VMEM((sets, seg_rows, half), BF16),
            pltpu.VMEM((seg_rows, half), F32),
            pltpu.VMEM((2, fold, chip_cols), BF16),
            pltpu.VMEM((sets, 2, seg_rows, fold), BF16),
            pltpu.VMEM((sets, 2, chips, seg_rows, fold), BF16),
            pltpu.VMEM((2, rows, fold), BF16),
            pltpu.VMEM((rows, chip_cols), F32),
            pltpu.VMEM((sets, 2, chips, seg_rows, own_cols), BF16),
            pltpu.VMEM((sets, groups, seg_rows, own_cols), BF16),
            pltpu.VMEM((sets, 2, chips, seg_rows, own_cols), BF16),
            pltpu.VMEM((sets, seg_rows, half), F32),
            pltpu.VMEM((seg_rows, half), F32),
            pltpu.VMEM((sets, seg_rows, half), BF16),
            pltpu.VMEM((micro, seg_rows, width), BF16),
            pltpu.VMEM((sets, seg_rows, half), BF16),
            pltpu.VMEM((2, sets, chips, seg_rows, own_cols), BF16),
            pltpu.VMEM((sets, 2, chips, seg_rows, own_cols), BF16),
            pltpu.VMEM((rows, chip_cols), BF16),
            pltpu.VMEM((micro, 2, rows, own_cols), BF16),
            pltpu.VMEM((sets, 2, chips, seg_rows, fold), BF16),
            pltpu.VMEM((sets, groups, seg_rows, fold), BF16),
            pltpu.VMEM((sets, seg_rows, half), BF16),
            pltpu.VMEM((sets, seg_rows, half), BF16),
            pltpu.VMEM((sets, seg_rows, 128), F32),
            pltpu.VMEM((micro, half, 2 * rows), BF16),
            pltpu.VMEM((seg_rows, fold), F32),
            pltpu.VMEM((1, half), F32),
            pltpu.VMEM((groups, 1, half), F32),
            pltpu.VMEM((1, width), F32),
            dma((4,)),
            dma((3,)),
            dma((sets,)),
            dma((sets, 2, len(gather_cuts) - 1)),
            dma((sets, 2)),
            dma((sets,)),
            dma((sets, 2)),
            dma((2, sets)),
            dma((sets, 2)),
            dma((sets, 2)),
            dma((sets, len(back_cuts) - 1)),
            dma((2, sets)),
            dma((2, sets)),
            dma((micro,)),
            dma((micro,)),
            dma((micro,)),
            dma((micro, 2)),
            dma((4,)),
            pltpu.SemaphoreType.REGULAR,
        ],
        compiler_params=pltpu.CompilerParams(
            collective_id=0, has_side_effects=True, vmem_limit_bytes=60 * 1024 * 1024
        ),
    )(flat_ids, acts_in, weights, gains, stored, cotangent)

    block_k = 1536
    blocks = width // block_k
    slot_count = stored.shape[1]

    def finish(
        ids_ref, normed_ref, slope_ref, stored_ref, arrived_ref, gain_ref,
        kept_ref, grad_ref, total_ref,
        normed_buf, slope_buf, kept_buf, arrived_buf, grad_buf, in_sem, out_sem, side_sem,
    ):
        side = [
            pltpu.make_async_copy(slope_ref, slope_buf, side_sem.at[0]),
            pltpu.make_async_copy(stored_ref, kept_buf, side_sem.at[1]),
            pltpu.make_async_copy(arrived_ref, arrived_buf, side_sem.at[2]),
            pltpu.make_async_copy(gain_ref, total_ref, side_sem.at[3]),
        ]
        places = [pl.ds(b * block_k, block_k) for b in range(blocks)]
        takes = [
            pltpu.make_async_copy(normed_ref.at[place], normed_buf.at[place], in_sem.at[b])
            for b, place in enumerate(places)
        ]
        gives = [
            pltpu.make_async_copy(grad_buf.at[place], grad_ref.at[0, place], out_sem.at[b])
            for b, place in enumerate(places)
        ]
        side[0].start()
        for take in takes:
            take.start()
        for copy in side[1:]:
            copy.start()
        side[0].wait()
        for place, take, give in zip(places, takes, gives):
            take.wait()
            grad_buf[place] = jnp.dot(
                normed_buf[place], slope_buf[...], preferred_element_type=F32
            )
            give.start()
        side[1].wait()
        side[2].wait()
        for m in range(micro):
            slot = ids_ref[m] - lax.axis_index("dp") * slot_count
            kept_buf[0, jnp.clip(slot, 0, slot_count - 1)] = arrived_buf[m]
        kept_copy = pltpu.make_async_copy(kept_buf, kept_ref, side_sem.at[4])
        kept_copy.start()
        side[3].wait()
        kept_copy.wait()
        for give in gives:
            give.wait()

    kept, grad, gain = pl.pallas_call(
        finish,
        out_shape=(
            jax.ShapeDtypeStruct(stored.shape, BF16),
            jax.ShapeDtypeStruct((1, width, own_cols), F32),
            jax.ShapeDtypeStruct((1, width), F32),
        ),
        in_specs=[smem] + [anywhere] * 5,
        out_specs=(anywhere,) * 3,
        scratch_shapes=[
            pltpu.VMEM(normed.shape, BF16),
            pltpu.VMEM(slope.shape, BF16),
            pltpu.VMEM(stored.shape, BF16),
            pltpu.VMEM(arrived.shape, BF16),
            pltpu.VMEM((width, own_cols), F32),
            dma((blocks,)),
            dma((blocks,)),
            dma((5,)),
        ],
        compiler_params=pltpu.CompilerParams(vmem_limit_bytes=60 * 1024 * 1024),
    )(flat_ids, normed, slope, stored, arrived, gain)
    return (kept, grad, gain)


def solution(mesh):
    placed = (
        P(None, "dp", None),
        P("section", None, "dp"),
        P("section", None),
        P("section", "dp", None, None),
        P(None, "dp"),
        P(None, "dp", None),
    )
    return jax.shard_map(
        functools.partial(on_device, mesh.shape["section"], mesh.shape["dp"]),
        mesh=mesh,
        in_specs=placed,
        out_specs=(P("section", "dp", None, None), P("section", None, "dp"), P("section", None)),
        check_vma=False,
    )
```

```python
import functools

import jax
import jax.numpy as jnp
from jax import lax
from jax.experimental import pallas as pl
from jax.experimental.pallas import tpu as pltpu
from jax.sharding import PartitionSpec as P

MESH = pl.DeviceIdType.MESH
F32 = jnp.float32
BF16 = jnp.bfloat16

clip_limit = 1.0
epsilon = 1e-05
gelu_coeff = 0.7978845608028654


def gelu_value(values):
    inner = gelu_coeff * (values + 0.044715 * values * values * values)
    return 0.5 * values * (1.0 + jnp.tanh(inner))


def gelu_slope(values):
    tangent = jnp.tanh(gelu_coeff * (values + 0.044715 * values * values * values))
    return 0.5 * (1.0 + tangent) + 0.5 * values * (1.0 - tangent * tangent) * gelu_coeff * (
        1.0 + 0.134145 * values * values
    )


device_steps = ((2, 1, 1), (2, 1, 0), (1, 1, 1), (1, 1, 0), (3, 1, 1), (3, 1, 0), (2, 0, 1), (2, 0, 0), (0, 1, 1), (0, 1, 0), (1, 0, 1), (1, 0, 0), (3, 0, 1), (3, 0, 0), (0, 0, 1))
gather_cuts = (0, 768, 1280, 1536)
back_cuts = (0, 512, 1024, 1536)
step_b = 256
plain_us = (3.5, 5.5, 2.8, 6.4, 0.0)
turning_us = (3.5, 5.5, 1.4, 6.4, 0.0)


def make_order(micro, turning, side):
    FR, FC, BC, BR, TN = range(5)
    stagger_us, gather_us, pair_us, back_us, late_us = turning_us if turning else plain_us
    events = []
    for k in range(4 * micro):
        start = stagger_us * k
        back = start + gather_us + pair_us if turning else start + 1000.0
        events.append((start + gather_us, FC * 8 + k))
        events.append((back, BC * 8 + k))
        if k % 2 == side:
            events.append((start + (late_us if k >= 4 else 0.0), FR * 8 + k))
            events.append((back + back_us, BR * 8 + k))
    for m in range(micro):
        events.append((2000.0 if turning else 500.0, TN * 8 + 4 * m))
    return [entry for _, entry in sorted(events)]


def relay(
    sections,
    groups,
    ids,
    acts_hbm,
    weights,
    gains_hbm,
    stored_hbm,
    cotangent_hbm,
    arrived_out,
    normed_out,
    slope_out,
    gain_out,
    acts,
    gains,
    stored,
    cotangent,
    acts_p,
    before_p,
    cotangent_p,
    gains_p,
    wbuf,
    nbuf,
    gbuf,
    xbuf,
    products,
    pout,
    pin,
    pair_in,
    hidden,
    incoming,
    arrived,
    arrived_whole,
    arr_in,
    slopes,
    slope_in,
    ybuf,
    own_slope,
    back_out,
    back_in,
    up_in,
    up_out,
    scales,
    xturned,
    gain_sum,
    gain_row,
    gain_in,
    gain_full,
    load_sem,
    w_sem,
    gather_send,
    gather_recv,
    part_send,
    part_recv,
    pair_recv,
    slope_send,
    slope_recv,
    back_send,
    back_recv,
    side_send,
    side_recv,
    keep_send,
    keep_recv,
    keep_sem,
    copy_sem,
    gain_sem,
    stagger,
):
    micro, seg_rows, width = acts.shape
    half = width // 2
    fold = half // 2
    own_cols = weights.shape[2]
    chip_cols = 2 * own_cols
    chips = groups // 2
    quarter = chips // 2
    rows = chips * seg_rows
    slot_count = stored.shape[1]
    sets = 2 * micro
    gather_parts = list(zip(gather_cuts[:-1], gather_cuts[1:]))
    back_parts = list(zip(back_cuts[:-1], back_cuts[1:]))
    section = lax.axis_index("section")
    me = lax.axis_index("dp")
    core = lax.rem(me, 2)
    chip = lax.div(me, 2)
    sibling = me + 1 - 2 * core
    first = section == 0
    last = section == sections - 1
    after = lax.rem(section + 1, sections)
    before = lax.rem(section + sections - 1, sections)
    z_count = groups // 4
    z_pos = lax.div(me, 4)
    x_pos = lax.rem(chip, 2)

    loads = [
        pltpu.make_async_copy(source, target, load_sem.at[i])
        for i, (source, target) in enumerate(
            (
                (acts_hbm, acts),
                (stored_hbm, stored),
                (gains_hbm, gains),
                (cotangent_hbm, cotangent),
            )
        )
    ]
    for load in loads:
        load.start()
    own_place = pl.ds(pl.multiple_of(core * own_cols, 128), own_cols)

    def weight_pieces(side):
        for q in range(quarter):
            for h in range(2):
                yield (
                    weights.at[
                        0, pl.ds(side * half + q * chip_cols + h * own_cols, own_cols), :
                    ],
                    wbuf.at[h, q * own_cols : (q + 1) * own_cols, own_place],
                )

    for source, target in weight_pieces(core):
        pltpu.make_async_copy(source, target, w_sem.at[2]).start()

    barrier = pltpu.get_barrier_semaphore()

    def greet(step, carry):
        other = lax.rem(me + step, groups)
        for there in (after, before):
            pl.semaphore_signal(
                barrier, inc=1, device_id={"section": there, "dp": other}, device_id_type=MESH
            )

        @pl.when(step > 0)
        def _():
            pl.semaphore_signal(
                barrier, inc=1, device_id={"section": section, "dp": other}, device_id_type=MESH
            )

        return carry

    lax.fori_loop(0, groups, greet, 0)

    def part(q):
        return slice(q * own_cols, (q + 1) * own_cols)

    def low_rows(shape):
        return lax.broadcasted_iota(jnp.int32, shape, len(shape) - 2) < 4

    def turned(value):
        return pltpu.roll(value, 4, axis=value.ndim - 2)

    def columns(q, h):
        start = q * chip_cols + h * own_cols
        return slice(start, start + own_cols)

    def pack(value, target, index):
        for q in range(chips):
            left, right = value[:, columns(q, 0)], value[:, columns(q, 1)]
            low = low_rows(left.shape)
            target[index, :, part(q)] = jnp.where(low, left, turned(right)).astype(target.dtype)
            target[index + 1, :, part(q)] = jnp.where(low, turned(left), right).astype(
                target.dtype
            )

    def unpack(one, two):
        low = low_rows(one.shape)
        return jnp.where(low, one, turned(two)), jnp.where(low, turned(one), two)

    for load in loads:
        load.wait()
    for q in range(chips):
        left = jnp.broadcast_to(gains[:, columns(q, 0)], (seg_rows, own_cols))
        right = jnp.broadcast_to(gains[:, columns(q, 1)], (seg_rows, own_cols))
        gains_p[:, part(q)] = jnp.where(low_rows(left.shape), left, right)
    for m in range(micro):
        slot = jnp.clip(ids[m] - me * slot_count, 0, slot_count - 1)
        pack(acts[m].astype(F32), acts_p, 2 * m)
        pack(stored[0, slot].astype(F32), before_p, 2 * m)
        pack(cotangent[m].astype(F32), cotangent_p, 2 * m)
    gain_sum[...] = jnp.zeros_like(gain_sum)
    pl.semaphore_wait(barrier, 3 * groups - 1)

    def remote(source, target, send, recv, there, other):
        return pltpu.make_async_remote_copy(
            src_ref=source,
            dst_ref=target,
            send_sem=send,
            recv_sem=recv,
            device_id={"section": there, "dp": other},
            device_id_type=MESH,
        )

    for source, target in weight_pieces(1 - core):
        remote(source, target, w_sem.at[0], w_sem.at[1], section, sibling).start()

    def far_z(i):
        away = jnp.where(i == 3, 0, jnp.where(i == 0, 2, 2 * i - 1))
        return lax.rem(z_pos + away, z_count)

    def far_device(i):
        if isinstance(i, int):
            z, x, c = device_steps[i]
            return (
                lax.rem(z_pos + z, z_count) * 4
                + lax.rem(x_pos + x, 2) * 2
                + lax.rem(core + c, 2)
            )
        x = lax.rem(x_pos + 1 - lax.rem(lax.div(i, 2), 2), 2)
        return far_z(lax.div(i, 4)) * 4 + x * 2 + lax.rem(core + 1 - lax.rem(i, 2), 2)

    def far_chip(i):
        return far_z(lax.div(i, 2)) * 2 + lax.rem(x_pos + 1 - lax.rem(i, 2), 2)

    def await_bytes(ref, sem):
        pltpu.make_async_copy(ref, ref, sem).wait()

    def row_mean(value):
        total = jnp.broadcast_to(jnp.sum(value, axis=-1, keepdims=True), (seg_rows, 128))
        return ((total + turned(total)) / width)[:, :1]

    def turned_place(m):
        wide = 2 * rows
        return (
            pl.ds(pl.multiple_of(core * half, half), half),
            pl.ds(pl.multiple_of(m * wide, wide), wide),
        )

    def keep_share(m):
        return remote(
            xturned.at[m],
            normed_out.at[turned_place(m)],
            keep_send.at[m],
            keep_recv.at[m],
            section,
            sibling,
        )

    def keep_own(m):
        return pltpu.make_async_copy(xturned.at[m], normed_out.at[turned_place(m)], keep_sem.at[m])

    def turn_normed(m):
        for q in range(quarter):
            sides = [[], []]
            for chain in range(2):
                one, two = (
                    gbuf[2 * m + u, chain, :, :, part(q)].astype(F32)
                    for u in range(2)
                )
                for h, whole in enumerate(unpack(one, two)):
                    sides[h].append(whole.reshape(rows, own_cols))
            for h in range(2):
                piece = jnp.transpose(jnp.concatenate(sides[h], axis=0))
                xturned[m, columns(q, h), :] = piece.astype(BF16)
        keep_share(m).start()
        keep_own(m).start()

    def slope_copy(m, chain):
        return pltpu.make_async_copy(
            own_slope.at[m, chain],
            slope_out.at[pl.ds(pl.multiple_of((m * 2 + chain) * rows, rows), rows), :],
            copy_sem.at[m, chain],
        )

    def send_shares(e):
        def send(step, carry):
            other = far_device(step)
            remote(
                slopes.at[1, e, lax.div(other, 2)],
                slope_in.at[e, core, chip],
                slope_send.at[1, e],
                slope_recv.at[e, core],
                section,
                other,
            ).start()
            return carry

        lax.fori_loop(0, groups - 1, send, 0)
        pltpu.make_async_copy(
            slopes.at[1, e, chip], slope_in.at[e, core, chip], slope_recv.at[e, core]
        ).start()

    @pl.when(last)
    def _():
        def share(e, carry):
            for q in range(chips):
                slopes[1, e, q] = cotangent_p[e, :, part(q)]
            send_shares(e)
            return carry

        lax.fori_loop(0, sets, share, 0)

    def pair_copy(e, chain):
        return remote(
            pout.at[e, chain],
            pair_in.at[e, chain],
            part_send.at[e, chain],
            pair_recv.at[e, chain],
            section,
            sibling,
        )

    def forward_rows(e):
        @pl.when(first & (e == 0) & (core == 1))
        def _():
            pl.semaphore_wait(stagger, 1)

        @pl.when(first)
        def _():
            incoming[...] = acts_p[e]

        @pl.when(jnp.logical_not(first))
        def _():
            await_bytes(arr_in.at[e], side_recv.at[0, e])
            await_bytes(pin.at[e], part_recv.at[e])
            for q in range(chips):
                value = pin[e, 2 * q].astype(F32) + pin[e, 2 * q + 1].astype(F32)
                hidden[e, :, part(q)] = value
                total = arr_in[e, :, part(q)].astype(F32) + gelu_value(value)
                incoming[:, part(q)] = total.astype(BF16).astype(F32)

        previous = before_p[e]
        moved = jnp.clip(incoming[...] - previous, -clip_limit, clip_limit)
        arrived_now = (previous + moved).astype(BF16)
        arrived[e] = arrived_now
        arrived_f = arrived_now.astype(F32)
        scale = lax.rsqrt(row_mean(arrived_f * arrived_f) + epsilon)
        scales[e] = jnp.broadcast_to(scale, (seg_rows, 128))
        normed = (arrived_f * scale * gains_p[...]).astype(BF16)
        for side in range(2):
            nbuf[e, side] = normed[:, side * fold : (side + 1) * fold]
        for p, (low_end, high_end) in enumerate(gather_parts):
            cut = slice(low_end, high_end)

            def send(step, carry, p=p, cut=cut):
                other = far_device(step)
                remote(
                    nbuf.at[e, lax.rem(other, 2), :, cut],
                    gbuf.at[e, core, chip, :, cut],
                    gather_send.at[e],
                    gather_recv.at[e, core, p],
                    section,
                    other,
                ).start()
                return carry

            for step in range(groups - 1):
                send(step, 0)
            pltpu.make_async_copy(
                nbuf.at[e, core, :, cut],
                gbuf.at[e, core, chip, :, cut],
                gather_recv.at[e, core, p],
            ).start()

        @pl.when(jnp.logical_not(last))
        def _():
            remote(
                arrived.at[e], arr_in.at[e], side_send.at[0, e], side_recv.at[0, e], after, me
            ).start()

        @pl.when(jnp.logical_not(first))
        def _():
            for q in range(chips):
                hidden[e, :, part(q)] = gelu_slope(hidden[e, :, part(q)])

    def forward_columns(e, chain):
        @pl.when((e == 0) & (chain == 0))
        def _():
            await_bytes(wbuf.at[:, :, own_place], w_sem.at[2])
            await_bytes(wbuf.at[:, :, own_place], w_sem.at[1])

        for p, (base, high_end) in enumerate(gather_parts):
            await_bytes(gbuf.at[e, chain, :, :, base:high_end], gather_recv.at[e, chain, p])
            if p == 0:

                @pl.when(first & (e == 0) & (chain == 0) & (core == 0))
                def _():
                    pl.semaphore_signal(
                        stagger, inc=1, device_id={"dp": sibling}, device_id_type=MESH
                    )

            piece = gbuf[e, chain, :, :, base:high_end].astype(F32)
            xbuf[:, base:high_end] = piece.reshape(rows, high_end - base).astype(BF16)
            for h in range(2):
                for c in range(0, chip_cols, 256):
                    product = jnp.dot(
                        xbuf[:, base:high_end],
                        wbuf[h, base:high_end, c : c + 256],
                        preferred_element_type=F32,
                    )
                    if p > 0:
                        product = product + products[h, :, c : c + 256]
                    products[h, :, c : c + 256] = product
        shape = (chips, seg_rows, own_cols)
        left = products[0, :, :own_cols].reshape(shape) + turned(
            products[1, :, :own_cols].reshape(shape)
        )
        right = (
            turned(products[0, :, own_cols:].reshape(shape))
            + products[1, :, own_cols:].reshape(shape)
        )
        pout[e, chain] = jnp.where(low_rows(shape), left, right).astype(BF16)

        def send(step, carry):
            q = far_chip(step)
            other = 2 * q + chain

            remote(
                pout.at[e, chain, q],
                pin.at[e, me],
                part_send.at[e, chain],
                part_recv.at[e],
                after,
                other,
            ).start()
            return carry

        @pl.when(jnp.logical_not(last))
        def _():
            lax.fori_loop(0, chips, send, 0, unroll=True)

        @pl.when(last)
        def _():
            pair_copy(e, chain).start()

    def backward_columns(e, chain):
        await_bytes(slope_in.at[e, chain], slope_recv.at[e, chain])

        @pl.when(last)
        def _():
            pair_copy(e, chain).wait_recv()
            value = pout[e, chain].astype(F32) + pair_in[e, chain].astype(F32)
            slope = slope_in[e, chain].astype(F32) * gelu_slope(value)
            slope_in[e, chain] = slope.astype(BF16)

        ybuf[...] = slope_in[e, chain].astype(F32).reshape(rows, own_cols).astype(BF16)
        for p, (low_end, high_end) in enumerate(back_parts):
            for start in range(low_end, high_end, step_b):
                shape = (chips, seg_rows, step_b)
                terms = [
                    [
                        lax.dot_general(
                            ybuf[...],
                            wbuf[h, start : start + step_b, s * own_cols : (s + 1) * own_cols],
                            (((1,), (1,)), ((), ())),
                            preferred_element_type=F32,
                        ).reshape(shape)
                        for s in range(2)
                    ]
                    for h in range(2)
                ]
                left = terms[0][0] + turned(terms[0][1])
                right = turned(terms[1][0]) + terms[1][1]
                back_out[e, chain, :, :, start : start + step_b] = jnp.where(
                    low_rows(shape), left, right
                ).astype(BF16)

            cut = slice(low_end, high_end)

            def send(step, carry, p=p, cut=cut):
                q = far_chip(step)
                other = 2 * q + chain

                @pl.when(other != me)
                def _():
                    remote(
                        back_out.at[e, chain, q, :, cut],
                        back_in.at[e, me, :, cut],
                        back_send.at[e, chain],
                        back_recv.at[e, p],
                        section,
                        other,
                    ).start()

                return carry

            @pl.when(jnp.logical_not(first))
            def _(p=p, send=send):
                lax.fori_loop(0, chips, send, 0, unroll=True)

            @pl.when(jnp.logical_not(first) & (core == chain))
            def _(p=p, cut=cut):
                pltpu.make_async_copy(
                    back_out.at[e, chain, chip, :, cut],
                    back_in.at[e, me, :, cut],
                    back_recv.at[e, p],
                ).start()

        for start in range(0, fold, 512):
            cut = slice(start, start + 512)
            term = back_out[e, chain, :, :, cut].astype(F32) * gbuf[e, chain, :, :, cut].astype(F32)
            gain_sum[:, cut] += jnp.sum(term, axis=0)

        @pl.when(lax.rem(e, 2) == 1)
        def _():
            m = lax.div(e, 2)
            left, right = unpack(
                slope_in[e - 1, chain].astype(F32), slope_in[e, chain].astype(F32)
            )
            mine = jnp.where(core == 0, left, right).reshape(rows, own_cols)
            own_slope[m, chain] = mine.astype(BF16)
            slope_copy(m, chain).start()

    def backward_rows(e):
        @pl.when(last)
        def _():
            up_in[e] = cotangent_p[e]

        @pl.when(jnp.logical_not(last))
        def _():
            await_bytes(up_in.at[e], side_recv.at[1, e])

        for p, (low_end, high_end) in enumerate(back_parts):
            cut = slice(low_end, high_end)
            await_bytes(back_in.at[e, :, :, cut], back_recv.at[e, p])
            for side in range(2):
                total = back_in[e, side, :, cut].astype(F32)
                for q in range(1, chips):
                    total = total + back_in[e, 2 * q + side, :, cut].astype(F32)
                incoming[:, side * fold + low_end : side * fold + high_end] = total
        back = incoming[...]
        arrived_f = arrived[e].astype(F32)
        scale = scales[e][:, :1]
        weighted = back * gains_p[...]
        mean_term = row_mean(weighted * arrived_f)
        total = up_in[e].astype(F32) + scale * (weighted - arrived_f * scale * scale * mean_term)
        up_out[e] = total.astype(BF16)

        def send(step, carry):
            q = far_chip(step)
            place = pl.ds(pl.multiple_of(q * own_cols, 128), own_cols)
            slope = up_out[e, :, place].astype(F32) * hidden[e, :, place]
            slopes[0, e, q] = slope.astype(BF16)
            for c in range(2):
                remote(
                    slopes.at[0, e, q],
                    slope_in.at[e, core, chip],
                    slope_send.at[0, e],
                    slope_recv.at[e, core],
                    before,
                    2 * q + c,
                ).start()
            return carry

        lax.fori_loop(0, chips, send, 0, unroll=True)

        @pl.when(section > 1)
        def _():
            remote(
                up_out.at[e], up_in.at[e], side_send.at[1, e], side_recv.at[1, e], before, me
            ).start()

    FR, FC, BC, BR, TN, NO = range(6)
    orders = [[make_order(micro, where, side) for side in range(2)] for where in range(2)]
    length = max(len(order) for pair in orders for order in pair)
    for pair in orders:
        for order in pair:
            order += [NO * 8] * (length - len(order))

    def run(t, carry):
        now = NO * 8
        for i in range(length):
            here = jnp.where(
                last,
                jnp.where(core == 0, orders[1][0][i], orders[1][1][i]),
                jnp.where(core == 0, orders[0][0][i], orders[0][1][i]),
            )
            now = jnp.where(t == i, here, now)
        kind = lax.div(now, 8)
        e = lax.rem(lax.div(now, 2), sets)
        chain = lax.rem(now, 2)
        pl.when(kind == FR)(lambda: forward_rows(e))
        pl.when(kind == FC)(lambda: forward_columns(e, chain))
        pl.when(kind == BC)(lambda: backward_columns(e, chain))
        pl.when((kind == BR) & jnp.logical_not(first))(lambda: backward_rows(e))
        pl.when(kind == TN)(lambda: turn_normed(lax.div(e, 2)))
        return carry

    lax.fori_loop(0, length, run, 0)

    low = low_rows(gain_sum.shape)
    sums = gain_sum[...]
    left = jnp.sum(jnp.where(low, sums, 0.0), axis=0, keepdims=True)
    right = jnp.sum(jnp.where(low, 0.0, sums), axis=0, keepdims=True)
    own_gains = jnp.where(core == 0, gains[:, :half], gains[:, half:])
    for q in range(quarter):
        for h, value in enumerate((left, right)):
            gain_row[:, columns(q, h)] = value[:, part(q)] / own_gains[:, columns(q, h)]

    def gain_send(step, carry):
        other = far_device(step)
        remote(
            gain_row, gain_in.at[me], gain_sem.at[0], gain_sem.at[1], section, other
        ).start()
        return carry

    lax.fori_loop(0, groups - 1, gain_send, 0)
    pltpu.make_async_copy(gain_row, gain_in.at[me], gain_sem.at[1]).start()

    for m in range(micro):
        for q in range(chips):
            wholes = unpack(
                arrived[2 * m, :, part(q)].astype(F32), arrived[2 * m + 1, :, part(q)].astype(F32)
            )
            for h, whole in enumerate(wholes):
                arrived_whole[m, :, columns(q, h)] = whole.astype(BF16)
    arrived_copy = pltpu.make_async_copy(arrived_whole, arrived_out, gain_sem.at[2])
    arrived_copy.start()
    await_bytes(wbuf.at[:, :, own_place], w_sem.at[0])
    for e in range(sets):
        await_bytes(back_in.at[e, 0 : groups - 1], gather_send.at[e])
        for chain in range(2):
            await_bytes(pout.at[e, chain], part_send.at[e, chain])

            @pl.when(jnp.logical_not(first) & (core == chain))
            def _(e=e, chain=chain):
                await_bytes(back_out.at[e, chain, 0 : chips - 1], back_send.at[e, chain])

            @pl.when(jnp.logical_not(first) & (core != chain))
            def _(e=e, chain=chain):
                await_bytes(back_out.at[e, chain], back_send.at[e, chain])

        @pl.when(last)
        def _(e=e):
            await_bytes(pin.at[e, 0 : groups - 1], slope_send.at[1, e])

        @pl.when(jnp.logical_not(first))
        def _(e=e):
            await_bytes(pin.at[e], slope_send.at[0, e])

        @pl.when(section > 1)
        def _(e=e):
            await_bytes(up_out.at[e], side_send.at[1, e])

        @pl.when(jnp.logical_not(last))
        def _(e=e):
            await_bytes(arrived.at[e], side_send.at[0, e])

    for m in range(micro):
        for chain in range(2):
            slope_copy(m, chain).wait()
        keep_share(m).wait()
        keep_own(m).wait()

    await_bytes(gain_in, gain_sem.at[1])
    for side in range(2):
        total = gain_in[side]
        for q in range(1, chips):
            total = total + gain_in[2 * q + side]
        gain_full[:, side * half : (side + 1) * half] = total
    await_bytes(gain_in.at[0 : groups - 1], gain_sem.at[0])
    gain_copy = pltpu.make_async_copy(gain_full, gain_out, gain_sem.at[3])
    gain_copy.start()
    arrived_copy.wait()
    gain_copy.wait()


def on_device(sections, groups, acts_in, weights, gains, stored, sample_ids, cotangent):
    micro, seg_rows, width = acts_in.shape
    own_cols = weights.shape[2]
    half = width // 2
    fold = half // 2
    chip_cols = 2 * own_cols
    chips = groups // 2
    rows = chips * seg_rows
    sets = 2 * micro
    flat_ids = sample_ids.reshape(micro)
    anywhere = pl.BlockSpec(memory_space=pl.ANY)
    smem = pl.BlockSpec(memory_space=pltpu.SMEM)
    dma = pltpu.SemaphoreType.DMA
    arrived, normed, slope, gain = pl.pallas_call(
        functools.partial(relay, sections, groups),
        out_shape=(
            jax.ShapeDtypeStruct((micro, seg_rows, width), BF16),
            jax.ShapeDtypeStruct((width, micro * 2 * rows), BF16),
            jax.ShapeDtypeStruct((micro * 2 * rows, own_cols), BF16),
            jax.ShapeDtypeStruct((1, width), F32),
        ),
        in_specs=[smem] + [anywhere] * 5,
        out_specs=(anywhere,) * 4,
        scratch_shapes=[
            pltpu.VMEM((micro, seg_rows, width), BF16),
            pltpu.VMEM((1, width), F32),
            pltpu.VMEM(stored.shape, BF16),
            pltpu.VMEM((micro, seg_rows, width), BF16),
            pltpu.VMEM((sets, seg_rows, half), F32),
            pltpu.VMEM((sets, seg_rows, half), F32),
            pltpu.VMEM((sets, seg_rows, half), BF16),
            pltpu.VMEM((seg_rows, half), F32),
            pltpu.VMEM((2, fold, chip_cols), BF16),
            pltpu.VMEM((sets, 2, seg_rows, fold), BF16),
            pltpu.VMEM((sets, 2, chips, seg_rows, fold), BF16),
            pltpu.VMEM((rows, fold), BF16),
            pltpu.VMEM((2, rows, chip_cols), F32),
            pltpu.VMEM((sets, 2, chips, seg_rows, own_cols), BF16),
            pltpu.VMEM((sets, groups, seg_rows, own_cols), BF16),
            pltpu.VMEM((sets, 2, chips, seg_rows, own_cols), BF16),
            pltpu.VMEM((sets, seg_rows, half), F32),
            pltpu.VMEM((seg_rows, half), F32),
            pltpu.VMEM((sets, seg_rows, half), BF16),
            pltpu.VMEM((micro, seg_rows, width), BF16),
            pltpu.VMEM((sets, seg_rows, half), BF16),
            pltpu.VMEM((2, sets, chips, seg_rows, own_cols), BF16),
            pltpu.VMEM((sets, 2, chips, seg_rows, own_cols), BF16),
            pltpu.VMEM((rows, own_cols), BF16),
            pltpu.VMEM((micro, 2, rows, own_cols), BF16),
            pltpu.VMEM((sets, 2, chips, seg_rows, fold), BF16),
            pltpu.VMEM((sets, groups, seg_rows, fold), BF16),
            pltpu.VMEM((sets, seg_rows, half), BF16),
            pltpu.VMEM((sets, seg_rows, half), BF16),
            pltpu.VMEM((sets, seg_rows, 128), F32),
            pltpu.VMEM((micro, half, 2 * rows), BF16),
            pltpu.VMEM((seg_rows, fold), F32),
            pltpu.VMEM((1, half), F32),
            pltpu.VMEM((groups, 1, half), F32),
            pltpu.VMEM((1, width), F32),
            dma((4,)),
            dma((3,)),
            dma((sets,)),
            dma((sets, 2, len(gather_cuts) - 1)),
            dma((sets, 2)),
            dma((sets,)),
            dma((sets, 2)),
            dma((2, sets)),
            dma((sets, 2)),
            dma((sets, 2)),
            dma((sets, len(back_cuts) - 1)),
            dma((2, sets)),
            dma((2, sets)),
            dma((micro,)),
            dma((micro,)),
            dma((micro,)),
            dma((micro, 2)),
            dma((4,)),
            pltpu.SemaphoreType.REGULAR,
        ],
        compiler_params=pltpu.CompilerParams(
            collective_id=0, has_side_effects=True, vmem_limit_bytes=60 * 1024 * 1024
        ),
    )(flat_ids, acts_in, weights, gains, stored, cotangent)

    block_k = 1536
    blocks = width // block_k
    slot_count = stored.shape[1]

    def finish(
        ids_ref, normed_ref, slope_ref, stored_ref, arrived_ref, gain_ref,
        kept_ref, grad_ref, total_ref,
        normed_buf, slope_buf, kept_buf, arrived_buf, grad_buf, in_sem, out_sem, side_sem,
    ):
        side = [
            pltpu.make_async_copy(slope_ref, slope_buf, side_sem.at[0]),
            pltpu.make_async_copy(stored_ref, kept_buf, side_sem.at[1]),
            pltpu.make_async_copy(arrived_ref, arrived_buf, side_sem.at[2]),
            pltpu.make_async_copy(gain_ref, total_ref, side_sem.at[3]),
        ]
        places = [pl.ds(b * block_k, block_k) for b in range(blocks)]
        takes = [
            pltpu.make_async_copy(normed_ref.at[place], normed_buf.at[place], in_sem.at[b])
            for b, place in enumerate(places)
        ]
        gives = [
            pltpu.make_async_copy(grad_buf.at[place], grad_ref.at[0, place], out_sem.at[b])
            for b, place in enumerate(places)
        ]
        side[0].start()
        for take in takes:
            take.start()
        for copy in side[1:]:
            copy.start()
        side[0].wait()
        for place, take, give in zip(places, takes, gives):
            take.wait()
            grad_buf[place] = jnp.dot(
                normed_buf[place], slope_buf[...], preferred_element_type=F32
            )
            give.start()
        side[1].wait()
        side[2].wait()
        for m in range(micro):
            slot = ids_ref[m] - lax.axis_index("dp") * slot_count
            kept_buf[0, jnp.clip(slot, 0, slot_count - 1)] = arrived_buf[m]
        kept_copy = pltpu.make_async_copy(kept_buf, kept_ref, side_sem.at[4])
        kept_copy.start()
        side[3].wait()
        kept_copy.wait()
        for give in gives:
            give.wait()

    kept, grad, gain = pl.pallas_call(
        finish,
        out_shape=(
            jax.ShapeDtypeStruct(stored.shape, BF16),
            jax.ShapeDtypeStruct((1, width, own_cols), F32),
            jax.ShapeDtypeStruct((1, width), F32),
        ),
        in_specs=[smem] + [anywhere] * 5,
        out_specs=(anywhere,) * 3,
        scratch_shapes=[
            pltpu.VMEM(normed.shape, BF16),
            pltpu.VMEM(slope.shape, BF16),
            pltpu.VMEM(stored.shape, BF16),
            pltpu.VMEM(arrived.shape, BF16),
            pltpu.VMEM((width, own_cols), F32),
            dma((blocks,)),
            dma((blocks,)),
            dma((5,)),
        ],
        compiler_params=pltpu.CompilerParams(vmem_limit_bytes=60 * 1024 * 1024),
    )(flat_ids, normed, slope, stored, arrived, gain)
    return (kept, grad, gain)


def solution(mesh):
    placed = (
        P(None, "dp", None),
        P("section", None, "dp"),
        P("section", None),
        P("section", "dp", None, None),
        P(None, "dp"),
        P(None, "dp", None),
    )
    return jax.shard_map(
        functools.partial(on_device, mesh.shape["section"], mesh.shape["dp"]),
        mesh=mesh,
        in_specs=placed,
        out_specs=(P("section", "dp", None, None), P("section", None, "dp"), P("section", None)),
        check_vma=False,
    )
```
